256 devices in a mesh: rep: 32 (over y, z_hi, core), tp: 8 (over x, z_lo).
Axes of the slice: x: 4, y: 4, z: 8 (z_hi: 4, z_lo: 2; z = z_hi * 2 + z_lo), core: 2. Of those that a mesh axis runs over, the one named last changes fastest.
Arguments:
- tokens: bfloat16 [32, 768, 4096], P('rep', 'tp'), may hold values from -400 to 400, as said below
- norm_gain: bfloat16 [32, 4096], P('rep'), may hold values from 0.25 to 1.75
- query_weight: bfloat16 [32, 4096, 2048], P('rep', None, 'tp'), may hold values from -0.0625 to 0.0625
- key_weight: bfloat16 [32, 4096, 1024], P('rep', None, 'tp'), may hold values from -2.8125 to 2.8125
- value_weight: bfloat16 [32, 4096, 1024], P('rep', None, 'tp'), may hold values from -0.09375 to 0.09375
- grad_out: bfloat16 [32, 768, 2048], P('rep', None, 'tp'), may hold values from -16 to 16
- step_index: int32 [], replicated, may hold values from 0 to 63
Outputs:
- query_update: bfloat16 [32, 4096, 2048], P('rep', None, 'tp')
- key_update: bfloat16 [32, 4096, 1024], P('rep', None, 'tp')
- value_update: bfloat16 [32, 4096, 1024], P('rep', None, 'tp')
- gain_update: bfloat16 [32, 4096], P('rep')
The draws below stay inside these ranges and needn't reach their ends.
Inputs may be any that keep to these rules, and one draw needn't show every extreme that they name: Entries of tokens lie within the bounds given.
All inputs are finite; a program needn't handle non-finite values.
Results may differ from the reference program's by a relative error of at most 0.015.
The reference program's roundings to bfloat16 on the way count: a program that leaves them out, or rounds other values in their place, can miss the bound.
Values may be sent and summed in bfloat16 or wider, within the bound.
No kernel may reach another device: no remote copies, remote signals or barrier semaphores. Data moves between devices by JAX's collectives and lax.ppermute only.
A program may use at most 128 MiB of HBM per device.

```python
import math
import jax
import jax.numpy as jnp
from jax import lax

D = 4096
HEADS = 16
KV = 8
HD = 128
TOK = 768
REPS = 32
N_REP = 32


def draw_query_weight(key, part):
    key = jax.random.fold_in(key, 11)
    result = jnp.clip(jax.random.normal(key, (REPS, D, HEADS * HD), jnp.float32), -4.0, 4.0) / D ** 0.5
    return result.astype(jnp.bfloat16)


def draw_key_weight(key, part):
    key = jax.random.fold_in(key, 12)
    result = jnp.clip(jax.random.normal(key, (REPS, D, KV * HD), jnp.float32), -4.0, 4.0) / D ** 0.5
    return result.astype(jnp.bfloat16)


def draw_tokens(key, part):
    key = jax.random.fold_in(key, 13)
    parts = jax.random.split(key, 3)
    row_scale = jnp.exp(jax.random.uniform(parts[1], (REPS, TOK, 1), jnp.float32, 0.0, math.log(10.0)))
    col_scale = jnp.exp(jax.random.uniform(parts[2], (REPS, 1, D), jnp.float32, 0.0, math.log(10.0)))
    base = jnp.clip(jax.random.normal(parts[0], (REPS, TOK, D), jnp.float32), -4.0, 4.0)
    values = base * row_scale * col_scale
    return values.astype(jnp.bfloat16)


def draw_grad_out(key, part):
    key = jax.random.fold_in(key, 14)
    parts = jax.random.split(key, 2)
    head_pos = (lax.broadcasted_iota(jnp.int32, (1, 1, HEADS * HD), 2) // HD).astype(jnp.float32)
    rising = 1.0 + 2.0 * head_pos / (HEADS - 1)
    row_scale = jnp.exp(jax.random.uniform(parts[1], (REPS, TOK, 1), jnp.float32, 0.0, math.log(10.0)))
    base = jnp.clip(jax.random.normal(parts[0], (REPS, TOK, HEADS * HD), jnp.float32), -4.0, 4.0)
    return (0.1 * base * row_scale * rising).astype(jnp.bfloat16)


def block_scale(own_key, dims, shards, smallest, top_value):
    level = 1.0
    for position, blocks in shards:
        draws = jax.random.uniform(jax.random.fold_in(jax.random.fold_in(own_key, 6), position), (blocks,), jnp.float32, smallest / len(shards), top_value / len(shards))
        level = level * jnp.repeat(jnp.exp(draws), dims[position] // blocks).reshape((-1,) + (1,) * (len(dims) - 1 - position))
    return level


def centred(stream_key, dims, width, reach, pieces=(), kind=jnp.bfloat16):
    values = jax.random.normal(stream_key, dims, jnp.float32) * width
    if len(pieces) > 0:
        values = block_scale(stream_key, dims, pieces, -0.22, 0.18) * values
    return jnp.clip(values, min=-reach, max=reach).astype(kind)


def setup_inputs(seed: int = 0) -> dict:
    seeds = jax.random.split(jax.random.key(seed), 8)
    return {
        "tokens": draw_tokens(jax.random.fold_in(seeds[7], 71), 0),
        "norm_gain": jnp.clip(1.0 + 0.15 * jax.random.normal(seeds[1], (REPS, D), jnp.float32), 0.25, 1.75).astype(jnp.bfloat16),
        "query_weight": draw_query_weight(jax.random.fold_in(seeds[7], 71), 0),
        "key_weight": draw_key_weight(jax.random.fold_in(seeds[7], 71), 0),
        "value_weight": centred(seeds[4], (REPS, D, KV * HD), D ** -0.5, 0.09375, ((0, 32), (2, 8))),
        "grad_out": draw_grad_out(jax.random.fold_in(seeds[7], 71), 0),
        "step_index": jax.random.randint(seeds[6], (), 0, 64).astype(jnp.int32),
    }


EPS = 1e-05

def replica_grads(operands):
    tokens, norm_gain, query_weight, key_weight, value_weight, grad_out = operands
    f32 = jnp.float32
    values = tokens.astype(f32)
    mean_square = lax.optimization_barrier(jnp.mean(values * values, axis=1, keepdims=True))
    unit_rows = values * lax.rsqrt(mean_square + EPS)
    normed = (unit_rows * norm_gain.astype(f32)).astype(jnp.bfloat16)
    query_rows = jnp.dot(normed, query_weight, preferred_element_type=f32).astype(jnp.bfloat16)
    key_rows = jnp.dot(normed, key_weight, preferred_element_type=f32).astype(jnp.bfloat16)
    value_rows = jnp.dot(normed, value_weight, preferred_element_type=f32).astype(jnp.bfloat16)
    seq_len = tokens.shape[0]
    kv_heads = key_weight.shape[1] // HD
    group_size = query_weight.shape[1] // key_weight.shape[1]
    score_scale = HD ** (-0.5)
    query_heads = query_rows.astype(f32).reshape(seq_len, kv_heads, group_size, HD)
    key_heads = key_rows.astype(f32).reshape(seq_len, kv_heads, HD)
    value_heads = value_rows.astype(f32).reshape(seq_len, kv_heads, HD)
    scores = jnp.einsum('tgjd,sgd->gjts', query_heads, key_heads) * score_scale
    row_index = lax.broadcasted_iota(jnp.int32, (seq_len, seq_len), 0)
    col_index = lax.broadcasted_iota(jnp.int32, (seq_len, seq_len), 1)
    scores = jnp.where(row_index >= col_index, scores, -1e+30)
    soft_weights = jnp.exp(scores - lax.optimization_barrier(jnp.max(scores, axis=-1, keepdims=True)))
    soft_weights = soft_weights / lax.optimization_barrier(jnp.sum(soft_weights, axis=-1, keepdims=True))
    soft_low = soft_weights.astype(jnp.bfloat16)
    upstream = grad_out.astype(f32).reshape(seq_len, kv_heads, group_size, HD)
    value_grad = jnp.einsum('gjts,tgjd->sgd', soft_low.astype(f32), upstream)
    value_grad = value_grad.reshape(seq_len, kv_heads * HD).astype(jnp.bfloat16)
    prob_grad = jnp.einsum('tgjd,sgd->gjts', upstream, value_heads)
    score_grad = soft_weights * (prob_grad - lax.optimization_barrier(jnp.sum(soft_weights * prob_grad, axis=-1, keepdims=True))) * score_scale
    score_grad = score_grad.astype(jnp.bfloat16).astype(f32)
    query_grad = jnp.einsum('gjts,sgd->tgjd', score_grad, key_heads).reshape(seq_len, -1).astype(jnp.bfloat16)
    key_grad = jnp.einsum('gjts,tgjd->sgd', score_grad, query_heads).reshape(seq_len, -1).astype(jnp.bfloat16)
    grad_query = jnp.dot(normed.T, query_grad, preferred_element_type=f32).astype(jnp.bfloat16)
    grad_key = jnp.dot(normed.T, key_grad, preferred_element_type=f32).astype(jnp.bfloat16)
    grad_value = jnp.dot(normed.T, value_grad, preferred_element_type=f32).astype(jnp.bfloat16)
    normed_grad = jnp.dot(query_grad, query_weight.T, preferred_element_type=f32)
    normed_grad = normed_grad + jnp.dot(key_grad, key_weight.T, preferred_element_type=f32)
    normed_grad = normed_grad + jnp.dot(value_grad, value_weight.T, preferred_element_type=f32)
    grad_gain = lax.optimization_barrier(jnp.sum(normed_grad * unit_rows, axis=0)).astype(jnp.bfloat16)
    return (grad_query, grad_key, grad_value, grad_gain)

def average_pair(own, other):
    return (0.5 * (own.astype(jnp.float32) + other.astype(jnp.float32))).astype(jnp.bfloat16)

def reference(tokens, norm_gain, query_weight, key_weight, value_weight, grad_out, step_index):
    grads = lax.map(replica_grads, (tokens, norm_gain, query_weight, key_weight, value_weight, grad_out))
    shift_bit = jnp.mod(step_index, 4).astype(jnp.int32)
    partner = jnp.bitwise_xor(jnp.arange(N_REP, dtype=jnp.int32), jnp.left_shift(jnp.int32(1), shift_bit))
    return (average_pair(grads[0], grads[0][partner]), average_pair(grads[1], grads[1][partner]), average_pair(grads[2], grads[2][partner]), average_pair(grads[3], grads[3][partner]))
```

```python
from functools import partial

import jax
import jax.numpy as jnp
from jax import lax
from jax.experimental import pallas as pl
from jax.experimental.pallas import tpu as pltpu
from jax.sharding import PartitionSpec as P

HD = 128
EPS = 1e-05
X_RING = 4
F32 = jnp.float32
BF16 = jnp.bfloat16
VMEM_LIMIT = 56 * 1024 * 1024


def tp_of(x, z):
    return (x % X_RING) * 2 + z


ROUTES = {
    "left": [(tp_of(x, z), tp_of(x + 1, z)) for x in range(X_RING) for z in range(2)],
    "right": [(tp_of(x, z), tp_of(x - 1, z)) for x in range(X_RING) for z in range(2)],
    "pair": [(tp_of(x, z), tp_of(x, 1 - z)) for x in range(X_RING) for z in range(2)],
}


def from_tp(block, side):
    return lax.ppermute(block, "tp", ROUTES[side])


def from_peer(block, bit):
    count = lax.axis_size("rep")
    return lax.ppermute(block, "rep", [(r, r ^ (1 << bit)) for r in range(count)])


def offset_of(dx, dz, rows):
    index = lax.axis_index("tp")
    x, z = index // 2, index % 2
    return (((x + dx) % X_RING) * 2 + (z + dz) % 2) * rows


def norm_kernel(tokens_ref, gain_ref, out_ref):
    values = tokens_ref[...].astype(F32)
    mean_square = jnp.mean(values * values, axis=1, keepdims=True)
    unit = values * lax.rsqrt(mean_square + EPS)
    out_ref[...] = (unit * gain_ref[...].astype(F32)).astype(BF16)


def normalize(tokens, gain):
    return pl.pallas_call(
        norm_kernel,
        out_shape=jax.ShapeDtypeStruct(tokens.shape, BF16),
        compiler_params=pltpu.CompilerParams(vmem_limit_bytes=VMEM_LIMIT),
        name="normalize",
    )(tokens, gain)


def project_kernel(count, *refs):
    pieces = refs[:count]
    wq_ref, wk_ref, wv_ref, out_ref, acc_ref = refs[count:]
    step = pl.program_id(0)
    rows = jnp.concatenate([p[...] for p in pieces], axis=0) if count > 1 else pieces[0][...]
    q_cols = wq_ref.shape[1]
    k_cols = wk_ref.shape[1]

    @pl.when(step == 0)
    def _():
        acc_ref[...] = jnp.zeros_like(acc_ref)

    acc_ref[:, :q_cols] += jnp.dot(rows, wq_ref[...], preferred_element_type=F32)
    weight_kv = jnp.concatenate([wk_ref[...], wv_ref[...]], axis=1)
    acc_ref[:, q_cols:] += jnp.dot(rows, weight_kv, preferred_element_type=F32)

    @pl.when(step == pl.num_programs(0) - 1)
    def _():
        out_ref[...] = acc_ref[...].astype(BF16)


def project(pieces, wq, wk, wv, tile=1024):
    width = wq.shape[0]
    rows = sum(p.shape[0] for p in pieces)
    cols = wq.shape[1] + wk.shape[1] + wv.shape[1]
    flops = 2 * rows * width * cols
    return pl.pallas_call(
        partial(project_kernel, len(pieces)),
        grid=(width // tile,),
        in_specs=[pl.BlockSpec((p.shape[0], tile), lambda i: (0, i)) for p in pieces]
        + [pl.BlockSpec((tile, w.shape[1]), lambda i: (i, 0)) for w in (wq, wk, wv)],
        out_specs=pl.BlockSpec((rows, cols), lambda i: (0, 0)),
        out_shape=jax.ShapeDtypeStruct((rows, cols), BF16),
        scratch_shapes=[pltpu.VMEM((rows, cols), F32)],
        compiler_params=pltpu.CompilerParams(vmem_limit_bytes=VMEM_LIMIT),
        cost_estimate=pl.CostEstimate(
            flops=flops, bytes_accessed=2 * (rows * width + width * cols), transcendentals=0
        ),
        name="project",
    )(*pieces, wq, wk, wv)


def attention_kernel(blocks, offs_ref, *refs):
    count = len(blocks)
    pieces = refs[:count]
    up_ref, out_ref, qkv_ref, dk_ref, dv_ref = refs[count:]
    seq = up_ref.shape[0]
    heads = up_ref.shape[1] // HD
    slot = 0
    for piece, parts in zip(pieces, blocks):
        at = 0
        for rows in parts:
            start = pl.multiple_of(offs_ref[slot], 32)
            qkv_ref[pl.ds(start, rows), :] = piece[at : at + rows, :]
            at += rows
            slot += 1
    scale = HD ** (-0.5)
    block = 256
    k_at = heads * HD
    v_at = k_at + HD
    for qb in range(seq // block):
        r0 = qb * block
        size = r0 + block
        keys = qkv_ref[:size, k_at : k_at + HD]
        values = qkv_ref[:size, v_at : v_at + HD]
        row = lax.broadcasted_iota(jnp.int32, (block, size), 0) + r0
        col = lax.broadcasted_iota(jnp.int32, (block, size), 1)
        keep = row >= col
        dk_part = None
        dv_part = None
        for h in range(heads):
            q = qkv_ref[r0:size, h * HD : (h + 1) * HD]
            up = up_ref[r0:size, h * HD : (h + 1) * HD]
            s = lax.dot_general(q, keys, (((1,), (1,)), ((), ())), preferred_element_type=F32)
            s = jnp.where(keep, s * scale, -1e30)
            p = jnp.exp(s - jnp.max(s, axis=1, keepdims=True))
            w = p * (1.0 / jnp.sum(p, axis=1, keepdims=True))
            low = w.astype(BF16)
            dp = lax.dot_general(up, values, (((1,), (1,)), ((), ())), preferred_element_type=F32)
            delta = jnp.sum(w * dp, axis=1, keepdims=True)
            ds = (w * (dp - delta) * scale).astype(BF16)
            dq = jnp.dot(ds, keys, preferred_element_type=F32)
            out_ref[r0:size, h * HD : (h + 1) * HD] = dq.astype(BF16)
            dk_h = lax.dot_general(ds, q, (((0,), (0,)), ((), ())), preferred_element_type=F32)
            dv_h = lax.dot_general(low, up, (((0,), (0,)), ((), ())), preferred_element_type=F32)
            dk_part = dk_h if dk_part is None else dk_part + dk_h
            dv_part = dv_h if dv_part is None else dv_part + dv_h
        if r0 > 0:
            dk_ref[:r0, :] += dk_part[:r0]
            dv_ref[:r0, :] += dv_part[:r0]
        dk_ref[r0:size, :] = dk_part[r0:]
        dv_ref[r0:size, :] = dv_part[r0:]
    out_ref[:, k_at : k_at + HD] = dk_ref[...].astype(BF16)
    out_ref[:, v_at : v_at + HD] = dv_ref[...].astype(BF16)


def attention(pieces, blocks, offs, up):
    seq = up.shape[0]
    cols = pieces[0].shape[1]
    vmem = pl.BlockSpec(memory_space=pltpu.VMEM)
    return pl.pallas_call(
        partial(attention_kernel, blocks),
        in_specs=[pl.BlockSpec(memory_space=pltpu.SMEM)] + [vmem] * (len(pieces) + 1),
        out_specs=vmem,
        out_shape=jax.ShapeDtypeStruct((seq, cols), BF16),
        scratch_shapes=[
            pltpu.VMEM((seq, cols), BF16),
            pltpu.VMEM((seq, HD), F32),
            pltpu.VMEM((seq, HD), F32),
        ],
        compiler_params=pltpu.CompilerParams(vmem_limit_bytes=VMEM_LIMIT),
        cost_estimate=pl.CostEstimate(
            flops=10 * 2 * seq * seq * HD, bytes_accessed=4 * seq * cols, transcendentals=seq * seq
        ),
        name="attention",
    )(offs, *pieces, up)


def fill_rows(offs_ref, pieces, rows_ref):
    for slot, piece in enumerate(pieces):
        start = pl.multiple_of(offs_ref[slot], 32)
        rows_ref[pl.ds(start, piece.shape[0]), :] = piece[...]


def own_grad_kernel(count, offs_ref, *refs):
    pieces = refs[:count]
    dqkv_ref, wq_ref, wk_ref, wv_ref, gain_ref = refs[count : count + 5]
    gq_ref, gk_ref, gv_ref, part_ref, rows_ref = refs[count + 5 :]
    fill_rows(offs_ref, pieces, rows_ref)
    grad = lax.dot_general(
        rows_ref[...], dqkv_ref[...], (((0,), (0,)), ((), ())), preferred_element_type=F32
    )
    q_cols = gq_ref.shape[1]
    k_at = q_cols
    v_at = q_cols + gk_ref.shape[1]
    gq_ref[...] = grad[:, :q_cols].astype(BF16)
    gk_ref[...] = grad[:, k_at:v_at].astype(BF16)
    gv_ref[...] = grad[:, v_at:].astype(BF16)
    folded = grad[:, k_at:v_at] * wk_ref[...].astype(F32) + grad[:, v_at:] * wv_ref[...].astype(F32)
    for c in range(0, q_cols, HD):
        folded = folded + grad[:, c : c + HD] * wq_ref[:, c : c + HD].astype(F32)
    total = jnp.sum(folded.T, axis=0, keepdims=True)
    part_ref[...] = total / gain_ref[...].astype(F32)


def own_grad(pieces, offs, dqkv, wq, wk, wv, gain, tile=512):
    seq, cols = dqkv.shape
    width = wq.shape[0]
    weights = (wq, wk, wv)
    outs = [jax.ShapeDtypeStruct(w.shape, BF16) for w in weights]
    w_specs = [pl.BlockSpec((tile, w.shape[1]), lambda i: (i, 0)) for w in weights]
    return pl.pallas_call(
        partial(own_grad_kernel, len(pieces)),
        grid=(width // tile,),
        in_specs=[pl.BlockSpec(memory_space=pltpu.SMEM)]
        + [pl.BlockSpec((p.shape[0], tile), lambda i: (0, i)) for p in pieces]
        + [pl.BlockSpec((seq, cols), lambda i: (0, 0))]
        + w_specs
        + [pl.BlockSpec((1, tile), lambda i: (0, i))],
        out_specs=w_specs + [pl.BlockSpec((1, tile), lambda i: (0, i))],
        out_shape=outs + [jax.ShapeDtypeStruct((1, width), F32)],
        scratch_shapes=[pltpu.VMEM((seq, tile), BF16)],
        compiler_params=pltpu.CompilerParams(vmem_limit_bytes=VMEM_LIMIT),
        cost_estimate=pl.CostEstimate(
            flops=2 * seq * width * cols,
            bytes_accessed=2 * (seq * width + 2 * width * cols),
            transcendentals=0,
        ),
        name="own_grad",
    )(offs, *pieces, dqkv, wq, wk, wv, gain)


def peer_grad_kernel(count, offs_ref, *refs):
    pieces = refs[:count]
    dqkv_ref, gq_ref, gk_ref, gv_ref = refs[count : count + 4]
    oq_ref, ok_ref, ov_ref, rows_ref = refs[count + 4 :]
    fill_rows(offs_ref, pieces, rows_ref)
    grad = lax.dot_general(
        rows_ref[...], dqkv_ref[...], (((0,), (0,)), ((), ())), preferred_element_type=F32
    )
    grad = grad.astype(BF16).astype(F32)
    q_cols = gq_ref.shape[1]
    v_at = q_cols + gk_ref.shape[1]
    oq_ref[...] = (0.5 * (gq_ref[...].astype(F32) + grad[:, :q_cols])).astype(BF16)
    ok_ref[...] = (0.5 * (gk_ref[...].astype(F32) + grad[:, q_cols:v_at])).astype(BF16)
    ov_ref[...] = (0.5 * (gv_ref[...].astype(F32) + grad[:, v_at:])).astype(BF16)


def peer_grad(pieces, offs, dqkv, grads, tile=512):
    seq, cols = dqkv.shape
    width = grads[0].shape[0]
    g_specs = [pl.BlockSpec((tile, g.shape[1]), lambda i: (i, 0)) for g in grads]
    return pl.pallas_call(
        partial(peer_grad_kernel, len(pieces)),
        grid=(width // tile,),
        in_specs=[pl.BlockSpec(memory_space=pltpu.SMEM)]
        + [pl.BlockSpec((p.shape[0], tile), lambda i: (0, i)) for p in pieces]
        + [pl.BlockSpec((seq, cols), lambda i: (0, 0))]
        + g_specs,
        out_specs=g_specs,
        out_shape=[jax.ShapeDtypeStruct(g.shape, BF16) for g in grads],
        scratch_shapes=[pltpu.VMEM((seq, tile), BF16)],
        compiler_params=pltpu.CompilerParams(vmem_limit_bytes=VMEM_LIMIT),
        cost_estimate=pl.CostEstimate(
            flops=2 * seq * width * cols,
            bytes_accessed=2 * (seq * width + 2 * width * cols),
            transcendentals=0,
        ),
        name="peer_grad",
    )(offs, *pieces, dqkv, *grads)


def thirds_of(block):
    third = block.shape[0] // 3
    return [block[i * third : (i + 1) * third] for i in range(3)]


def first_hop(own):
    return [from_tp(own, side) for side in ("left", "right", "pair")]


def second_hop(first):
    left, right, pair = first
    return [from_tp(pair, "left"), from_tp(right, "right"), from_tp(right, "pair")]


def last_hop(second):
    left, right, pair = second
    return [
        from_tp(thirds_of(left)[0], "left"),
        from_tp(thirds_of(pair)[1], "right"),
        from_tp(thirds_of(right)[2], "pair"),
    ]


def tp_sum(value):
    by_pair = value + from_tp(value, "pair")
    near = [(i, ((i // 2) ^ 1) * 2 + i % 2) for i in range(8)]
    far = [(i, ((i // 2) ^ 2) * 2 + i % 2) for i in range(8)]
    by_near = by_pair + lax.ppermute(by_pair, "tp", near)
    return by_near + lax.ppermute(by_near, "tp", far)


def branch(bit, normed, gain, wq, wk, wv, up):
    rows = normed.shape[0]
    first_at = [(-1, 0), (1, 0), (0, 1)]
    second_at = [(-1, 1), (2, 0), (1, 1)]
    offs = [offset_of(dx, dz, rows) for dx, dz in [(0, 0)] + first_at + second_at]
    last = offset_of(2, 1, rows)
    third = rows // 3
    offs = jnp.stack(offs + [last, last + third, last + 2 * third]).astype(jnp.int32)
    qkv_offs = offs[:8]

    peer_own = from_peer(normed, bit)
    first = first_hop(normed)
    own_rows = project([normed], wq, wk, wv)
    second = second_hop(first)
    first_rows = project(first, wq, wk, wv)
    final = last_hop(second)
    second_rows = project(second, wq, wk, wv)
    last_rows = project(final, wq, wk, wv)
    pieces = [normed] + first + second + final
    blocks = [[rows], [rows] * 3, [rows] * 3, [rows]]
    dqkv = attention([own_rows, first_rows, second_rows, last_rows], blocks, qkv_offs, up)
    peer_dqkv = from_peer(dqkv, bit)
    if bit == 0:
        peer_pieces = [peer_own] + [from_peer(p, bit) for p in first + second + final]
    else:
        peer_first = first_hop(peer_own)
        peer_second = second_hop(peer_first)
        peer_pieces = [peer_own] + peer_first + peer_second + last_hop(peer_second)
    *grads, part = own_grad(pieces, offs, dqkv, wq, wk, wv, gain)
    grad_gain = tp_sum(part).astype(BF16)
    peer_gain = from_peer(grad_gain, bit)
    outs = peer_grad(peer_pieces, offs, peer_dqkv, grads)
    gain_update = (0.5 * (grad_gain.astype(F32) + peer_gain.astype(F32))).astype(BF16)
    return tuple(outs) + (gain_update,)


def body(tokens, norm_gain, query_weight, key_weight, value_weight, grad_out, step_index):
    normed = normalize(tokens[0], norm_gain)
    outs = lax.switch(
        jnp.mod(step_index, 4),
        [partial(branch, bit) for bit in range(4)],
        normed,
        norm_gain,
        query_weight[0],
        key_weight[0],
        value_weight[0],
        grad_out[0],
    )
    return outs[0][None], outs[1][None], outs[2][None], outs[3]


def solution(mesh):
    in_specs = (
        P("rep", "tp", None),
        P("rep", None),
        P("rep", None, "tp"),
        P("rep", None, "tp"),
        P("rep", None, "tp"),
        P("rep", None, "tp"),
        P(),
    )
    out_specs = (P("rep", None, "tp"), P("rep", None, "tp"), P("rep", None, "tp"), P("rep", None))
    return jax.shard_map(body, mesh=mesh, in_specs=in_specs, out_specs=out_specs, check_vma=False)
```

```python
from functools import partial

import jax
import jax.numpy as jnp
from jax import lax
from jax.experimental import pallas as pl
from jax.experimental.pallas import tpu as pltpu
from jax.sharding import PartitionSpec as P

HD = 128
EPS = 1e-05
X_RING = 4
F32 = jnp.float32
BF16 = jnp.bfloat16
VMEM_LIMIT = 16 * 1024 * 1024


def tp_of(x, z):
    return (x % X_RING) * 2 + z


ROUTES = {
    "left": [(tp_of(x, z), tp_of(x + 1, z)) for x in range(X_RING) for z in range(2)],
    "right": [(tp_of(x, z), tp_of(x - 1, z)) for x in range(X_RING) for z in range(2)],
    "pair": [(tp_of(x, z), tp_of(x, 1 - z)) for x in range(X_RING) for z in range(2)],
}


def from_tp(block, side):
    return lax.ppermute(block, "tp", ROUTES[side])


def from_peer(block, bit):
    count = lax.axis_size("rep")
    return lax.ppermute(block, "rep", [(r, r ^ (1 << bit)) for r in range(count)])


def offset_of(dx, dz, rows):
    index = lax.axis_index("tp")
    x, z = index // 2, index % 2
    return (((x + dx) % X_RING) * 2 + (z + dz) % 2) * rows


def norm_kernel(tokens_ref, gain_ref, out_ref):
    values = tokens_ref[...].astype(F32)
    mean_square = jnp.mean(values * values, axis=1, keepdims=True)
    unit = values * lax.rsqrt(mean_square + EPS)
    out_ref[...] = (unit * gain_ref[...].astype(F32)).astype(BF16)


def normalize(tokens, gain):
    return pl.pallas_call(
        norm_kernel,
        out_shape=jax.ShapeDtypeStruct(tokens.shape, BF16),
        compiler_params=pltpu.CompilerParams(vmem_limit_bytes=VMEM_LIMIT),
        name="normalize",
    )(tokens, gain)


TILE = 256
WHOLE = pl.BlockSpec(memory_space=pltpu.VMEM)
LIGHT = pl.CostEstimate(flops=1, bytes_accessed=1, transcendentals=0)
PARAMS = pltpu.CompilerParams(vmem_limit_bytes=VMEM_LIMIT)


def project_kernel(count, *refs):
    pieces = refs[:count]
    wq_ref, wk_ref, wv_ref, out_ref = refs[count:]
    q_cols = wq_ref.shape[1]
    tile = 1024
    q_sum = None
    kv_sum = None
    for at in range(0, wq_ref.shape[0], tile):
        depth = slice(at, at + tile)
        rows = [p[:, depth] for p in pieces]
        rows = jnp.concatenate(rows, axis=0) if count > 1 else rows[0]
        weight_kv = jnp.concatenate([wk_ref[depth, :], wv_ref[depth, :]], axis=1)
        q_part = jnp.dot(rows, wq_ref[depth, :], preferred_element_type=F32)
        kv_part = jnp.dot(rows, weight_kv, preferred_element_type=F32)
        q_sum = q_part if q_sum is None else q_sum + q_part
        kv_sum = kv_part if kv_sum is None else kv_sum + kv_part
    out_ref[:, :q_cols] = q_sum.astype(BF16)
    out_ref[:, q_cols:] = kv_sum.astype(BF16)


def project(pieces, wq, wk, wv):
    rows = sum(p.shape[0] for p in pieces)
    cols = wq.shape[1] + wk.shape[1] + wv.shape[1]
    return pl.pallas_call(
        partial(project_kernel, len(pieces)),
        in_specs=[WHOLE] * (len(pieces) + 3),
        out_specs=WHOLE,
        out_shape=jax.ShapeDtypeStruct((rows, cols), BF16),
        compiler_params=PARAMS,
        cost_estimate=LIGHT,
        name="project",
    )(*pieces, wq, wk, wv)


def attention_kernel(blocks, offs_ref, *refs):
    count = len(blocks)
    pieces = refs[:count]
    up_ref, out_ref, qkv_ref, keys_t_ref, dk_ref, dv_ref = refs[count:]
    seq = up_ref.shape[0]
    heads = up_ref.shape[1] // HD
    slot = 0
    for piece, parts in zip(pieces, blocks):
        at = 0
        for rows in parts:
            start = pl.multiple_of(offs_ref[slot], 16)
            qkv_ref[pl.ds(start, rows), :] = piece[at : at + rows, :]
            at += rows
            slot += 1
    scale = HD ** (-0.5)
    block = TILE
    k_at = heads * HD
    v_at = k_at + HD
    keys_t_ref[...] = qkv_ref[:, k_at:v_at].T
    dk_ref[...] = jnp.zeros_like(dk_ref)
    dv_ref[...] = jnp.zeros_like(dv_ref)
    across = (((1,), (1,)), ((), ()))

    def head(h, carry):
        cols = pl.ds(pl.multiple_of(h * HD, HD), HD)
        for r0 in range(0, seq, block):
            size = r0 + block
            keys = qkv_ref[:size, k_at:v_at]
            values = qkv_ref[:size, v_at : v_at + HD]
            row = lax.broadcasted_iota(jnp.int32, (block, size), 0) + r0
            col = lax.broadcasted_iota(jnp.int32, (block, size), 1)
            q = qkv_ref[r0:size, cols]
            up = up_ref[r0:size, cols]
            s = lax.dot_general(q, keys, across, preferred_element_type=F32)
            s = jnp.where(row >= col, s * scale, -1e30)
            p = jnp.exp(s - jnp.max(s, axis=1, keepdims=True))
            w = p * (1.0 / jnp.sum(p, axis=1, keepdims=True))
            dp = lax.dot_general(up, values, across, preferred_element_type=F32)
            delta = jnp.sum(w * dp, axis=1, keepdims=True)
            ds = (w * (dp - delta) * scale).astype(BF16)
            dq = lax.dot_general(keys_t_ref[:, :size], ds, across, preferred_element_type=F32)
            out_ref[cols, r0:size] = dq.astype(BF16)
            dk_ref[:, :size] += jnp.dot(q.T, ds, preferred_element_type=F32)
            dv_ref[:, :size] += jnp.dot(up.T, w.astype(BF16), preferred_element_type=F32)
        return carry

    lax.fori_loop(0, heads, head, 0)
    out_ref[k_at:v_at, :] = dk_ref[...].astype(BF16)
    out_ref[v_at:, :] = dv_ref[...].astype(BF16)


def attention(pieces, blocks, offs, up):
    seq = up.shape[0]
    cols = pieces[0].shape[1]
    return pl.pallas_call(
        partial(attention_kernel, blocks),
        in_specs=[pl.BlockSpec(memory_space=pltpu.SMEM)] + [WHOLE] * (len(pieces) + 1),
        out_specs=WHOLE,
        out_shape=jax.ShapeDtypeStruct((cols, seq), BF16),
        scratch_shapes=[
            pltpu.VMEM((seq, cols), BF16),
            pltpu.VMEM((HD, seq), BF16),
            pltpu.VMEM((HD, seq), F32),
            pltpu.VMEM((HD, seq), F32),
        ],
        compiler_params=PARAMS,
        cost_estimate=LIGHT,
        name="attention",
    )(offs, *pieces, up)


def grad_tile(offs_ref, pieces, depth, dqkv_ref, rows_ref):
    for slot, piece in enumerate(pieces):
        start = pl.multiple_of(offs_ref[slot], 16)
        rows_ref[pl.ds(start, piece.shape[0]), :] = piece[:, depth]
    turned = jnp.dot(dqkv_ref[...], rows_ref[...], preferred_element_type=F32)
    return turned.astype(BF16).T.astype(F32)


def over_tiles(width, tile, one):
    def pair(j, carry):
        for k in range(2):
            one(pl.ds(pl.multiple_of((2 * j + k) * tile, tile), tile), k)
        return carry

    lax.fori_loop(0, width // (2 * tile), pair, 0)


def own_grad_kernel(count, waits, offs_ref, *refs):
    pieces = refs[:count]
    dqkv_ref, wq_ref, wk_ref, wv_ref, gain_ref = refs[count : count + 5]
    gq_ref, gk_ref, gv_ref, part_ref, rows_ref = refs[count + 5 + waits :]
    q_cols = gq_ref.shape[1]
    v_at = q_cols + gk_ref.shape[1]

    def one(depth, slot):
        grad = grad_tile(offs_ref, pieces, depth, dqkv_ref, rows_ref.at[slot])
        gq_ref[depth, :] = grad[:, :q_cols].astype(BF16)
        gk_ref[depth, :] = grad[:, q_cols:v_at].astype(BF16)
        gv_ref[depth, :] = grad[:, v_at:].astype(BF16)
        folded = grad[:, q_cols:v_at] * wk_ref[depth, :].astype(F32)
        folded = folded + grad[:, v_at:] * wv_ref[depth, :].astype(F32)
        for c in range(0, q_cols, HD):
            folded = folded + grad[:, c : c + HD] * wq_ref[depth, c : c + HD].astype(F32)
        total = jnp.sum(folded.T, axis=0, keepdims=True)
        part_ref[:, depth] = total / gain_ref[:, depth].astype(F32)

    over_tiles(gq_ref.shape[0], 2 * TILE, one)


def own_grad(pieces, offs, dqkv, wq, wk, wv, gain, earlier):
    seq = dqkv.shape[1]
    weights = (wq, wk, wv)
    outs = [jax.ShapeDtypeStruct(w.shape, BF16) for w in weights]
    return pl.pallas_call(
        partial(own_grad_kernel, len(pieces), len(earlier)),
        in_specs=[pl.BlockSpec(memory_space=pltpu.SMEM)]
        + [WHOLE] * (len(pieces) + 5 + len(earlier)),
        out_specs=[WHOLE] * 4,
        out_shape=outs + [jax.ShapeDtypeStruct((1, wq.shape[0]), F32)],
        scratch_shapes=[pltpu.VMEM((2, seq, 2 * TILE), BF16)],
        compiler_params=PARAMS,
        cost_estimate=LIGHT,
        name="own_grad",
    )(offs, *pieces, dqkv, wq, wk, wv, gain, *earlier)


def peer_grad_kernel(count, parts, offs_ref, *refs):
    pieces = refs[:count]
    dqkv_refs = refs[count : count + parts]
    gq_ref, gk_ref, gv_ref, oq_ref, ok_ref, ov_ref, rows_ref = refs[count + parts :]
    q_cols = gq_ref.shape[1]
    v_at = q_cols + gk_ref.shape[1]

    def one(depth, slot):
        dqkv = [r[...] for r in dqkv_refs]
        dqkv = jnp.concatenate(dqkv, axis=0) if parts > 1 else dqkv[0]
        grad = grad_tile(offs_ref, pieces, depth, dqkv, rows_ref.at[slot])
        oq_ref[depth, :] = (0.5 * (gq_ref[depth, :].astype(F32) + grad[:, :q_cols])).astype(BF16)
        ok_ref[depth, :] = (0.5 * (gk_ref[depth, :].astype(F32) + grad[:, q_cols:v_at])).astype(BF16)
        ov_ref[depth, :] = (0.5 * (gv_ref[depth, :].astype(F32) + grad[:, v_at:])).astype(BF16)

    over_tiles(gq_ref.shape[0], 2 * TILE, one)


def peer_grad(pieces, offs, dqkv, grads):
    seq = dqkv[0].shape[1]
    return pl.pallas_call(
        partial(peer_grad_kernel, len(pieces), len(dqkv)),
        in_specs=[pl.BlockSpec(memory_space=pltpu.SMEM)]
        + [WHOLE] * (len(pieces) + len(dqkv) + 3),
        out_specs=[WHOLE] * 3,
        out_shape=[jax.ShapeDtypeStruct(g.shape, BF16) for g in grads],
        scratch_shapes=[pltpu.VMEM((2, seq, 2 * TILE), BF16)],
        compiler_params=PARAMS,
        cost_estimate=LIGHT,
        name="peer_grad",
    )(offs, *pieces, *dqkv, *grads)


def first_hop(own):
    return [from_tp(own, side) for side in ("left", "right", "pair")]


def second_hop(first):
    left, right, pair = first
    return [from_tp(pair, "left"), from_tp(right, "right"), from_tp(right, "pair")]


def halves_of(block):
    half = block.shape[0] // 2
    return block[:half], block[half:]


def last_hop(second):
    left, _, pair = second
    return [from_tp(halves_of(left)[0], "left"), from_tp(halves_of(pair)[1], "right")]


def tp_sum(value):
    by_pair = value + from_tp(value, "pair")
    near = [(i, ((i // 2) ^ 1) * 2 + i % 2) for i in range(8)]
    far = [(i, ((i // 2) ^ 2) * 2 + i % 2) for i in range(8)]
    by_near = by_pair + lax.ppermute(by_pair, "tp", near)
    return by_near + lax.ppermute(by_near, "tp", far)


def after(value, *earlier):
    return lax.optimization_barrier((value, *earlier))[0]


def exchange(peer_bit, block):
    return lax.switch(peer_bit, [partial(from_peer, bit=bit) for bit in range(4)], block)


def body(tokens, norm_gain, query_weight, key_weight, value_weight, grad_out, step_index):
    wq, wk, wv, up = query_weight[0], key_weight[0], value_weight[0], grad_out[0]
    peer_bit = jnp.mod(step_index, 4)
    normed = normalize(tokens[0], norm_gain)
    rows = normed.shape[0]
    half = rows // 2
    q_cols = wq.shape[1]
    places = [(0, 0, 0), (-1, 0, 0), (1, 0, 0), (0, 1, 0), (-1, 1, 0), (2, 0, 0), (1, 1, 0)]
    places = places + [(2, 1, 0), (2, 1, half)]
    offs = jnp.stack([offset_of(x, z, rows) + at for x, z, at in places]).astype(jnp.int32)
    top, bottom = halves_of(normed)

    first = first_hop(normed)
    peer_top = exchange(peer_bit, top)
    go = after(first, peer_top)
    second = second_hop(go)
    rows_a = project([normed] + first, wq, wk, wv)
    peer_bottom = exchange(peer_bit, after(bottom, rows_a))
    peer_own = jnp.concatenate([peer_top, peer_bottom], axis=0)
    final = last_hop(after(second, peer_bottom))
    rows_b = project(second, wq, wk, wv)
    peer_first = first_hop(after(peer_own, *final))
    rows_c = project(after(final, rows_b), wq, wk, wv)
    blocks = [[rows] * 4, [rows] * 3, [half] * 2]
    dqkv = attention([rows_a, rows_b, rows_c], blocks, offs, up)
    peer_kv = exchange(peer_bit, dqkv[q_cols:])
    peer_second = second_hop(after(peer_first, peer_kv))
    peer_q = exchange(peer_bit, after(dqkv[:q_cols], peer_kv))
    pieces = [normed] + first + second + final
    *grads, part = own_grad(pieces, offs, dqkv, wq, wk, wv, norm_gain, [peer_q])
    peer_final = last_hop(after(peer_second, part))
    grad_gain = tp_sum(after(part, *peer_second)).astype(BF16)
    peer_gain = exchange(peer_bit, grad_gain)
    peer_pieces = [peer_own] + peer_first + peer_second + peer_final
    outs = peer_grad(peer_pieces, offs, [peer_q, peer_kv], grads)
    gain_update = (0.5 * (grad_gain.astype(F32) + peer_gain.astype(F32))).astype(BF16)
    return outs[0][None], outs[1][None], outs[2][None], gain_update


def solution(mesh):
    in_specs = (
        P("rep", "tp", None),
        P("rep", None),
        P("rep", None, "tp"),
        P("rep", None, "tp"),
        P("rep", None, "tp"),
        P("rep", None, "tp"),
        P(),
    )
    out_specs = (P("rep", None, "tp"), P("rep", None, "tp"), P("rep", None, "tp"), P("rep", None))
    return jax.shard_map(body, mesh=mesh, in_specs=in_specs, out_specs=out_specs, check_vma=False)
```

```python
from functools import partial

import jax
import jax.numpy as jnp
from jax import lax
from jax.experimental import pallas as pl
from jax.experimental.pallas import tpu as pltpu
from jax.sharding import PartitionSpec as P

HD = 128
EPS = 1e-05
X_RING = 4
F32 = jnp.float32
BF16 = jnp.bfloat16
VMEM_LIMIT = 16 * 1024 * 1024
TILE = 256
WHOLE = pl.BlockSpec(memory_space=pltpu.VMEM)
LIGHT = pl.CostEstimate(flops=1, bytes_accessed=1, transcendentals=0)
PARAMS = pltpu.CompilerParams(vmem_limit_bytes=VMEM_LIMIT)


def tp_of(x, z):
    return (x % X_RING) * 2 + z


ROUTES = {
    "left": [(tp_of(x, z), tp_of(x + 1, z)) for x in range(X_RING) for z in range(2)],
    "right": [(tp_of(x, z), tp_of(x - 1, z)) for x in range(X_RING) for z in range(2)],
    "pair": [(tp_of(x, z), tp_of(x, 1 - z)) for x in range(X_RING) for z in range(2)],
}


def from_tp(block, side):
    return lax.ppermute(block, "tp", ROUTES[side])


def from_peer(block, bit):
    count = lax.axis_size("rep")
    return lax.ppermute(block, "rep", [(r, r ^ (1 << bit)) for r in range(count)])


def offset_of(dx, dz, rows):
    index = lax.axis_index("tp")
    x, z = index // 2, index % 2
    return (((x + dx) % X_RING) * 2 + (z + dz) % 2) * rows


def norm_kernel(tokens_ref, gain_ref, out_ref, top_ref, bottom_ref):
    values = tokens_ref[...].astype(F32)
    mean_square = jnp.mean(values * values, axis=1, keepdims=True)
    unit = values * lax.rsqrt(mean_square + EPS)
    normed = (unit * gain_ref[...].astype(F32)).astype(BF16)
    half = top_ref.shape[0]
    out_ref[...] = normed
    top_ref[...] = normed[:half]
    bottom_ref[...] = normed[half:]


def normalize(tokens, gain):
    rows, width = tokens.shape
    shapes = [(rows, width), (rows // 2, width), (rows // 2, width)]
    return pl.pallas_call(
        norm_kernel,
        out_shape=[jax.ShapeDtypeStruct(shape, BF16) for shape in shapes],
        compiler_params=pltpu.CompilerParams(vmem_limit_bytes=VMEM_LIMIT),
        name="normalize",
    )(tokens, gain)


def join_kernel(top_ref, bottom_ref, out_ref):
    half = top_ref.shape[0]
    out_ref[:half, :] = top_ref[...]
    out_ref[half:, :] = bottom_ref[...]


def join(top, bottom):
    return pl.pallas_call(
        join_kernel,
        in_specs=[WHOLE] * 2,
        out_specs=WHOLE,
        out_shape=jax.ShapeDtypeStruct((2 * top.shape[0], top.shape[1]), BF16),
        compiler_params=PARAMS,
        cost_estimate=LIGHT,
        name="join",
    )(top, bottom)


def project_kernel(count, *refs):
    pieces = refs[:count]
    wq_ref, wk_ref, wv_ref, out_ref = refs[count:]
    q_cols = wq_ref.shape[1]
    tile = 1024
    q_sum = None
    kv_sum = None
    for at in range(0, wq_ref.shape[0], tile):
        depth = slice(at, at + tile)
        rows = [p[:, depth] for p in pieces]
        rows = jnp.concatenate(rows, axis=0) if count > 1 else rows[0]
        weight_kv = jnp.concatenate([wk_ref[depth, :], wv_ref[depth, :]], axis=1)
        q_part = jnp.dot(rows, wq_ref[depth, :], preferred_element_type=F32)
        kv_part = jnp.dot(rows, weight_kv, preferred_element_type=F32)
        q_sum = q_part if q_sum is None else q_sum + q_part
        kv_sum = kv_part if kv_sum is None else kv_sum + kv_part
    out_ref[:, :q_cols] = q_sum.astype(BF16)
    out_ref[:, q_cols:] = kv_sum.astype(BF16)


def project(pieces, wq, wk, wv):
    rows = sum(p.shape[0] for p in pieces)
    cols = wq.shape[1] + wk.shape[1] + wv.shape[1]
    return pl.pallas_call(
        partial(project_kernel, len(pieces)),
        in_specs=[WHOLE] * (len(pieces) + 3),
        out_specs=WHOLE,
        out_shape=jax.ShapeDtypeStruct((rows, cols), BF16),
        compiler_params=PARAMS,
        cost_estimate=LIGHT,
        name="project",
    )(*pieces, wq, wk, wv)


def attention_kernel(blocks, offs_ref, *refs):
    count = len(blocks)
    pieces = refs[:count]
    up_ref, out_ref, kv_ref, qkv_ref, keys_t_ref, dk_ref, dv_ref = refs[count:]
    seq = up_ref.shape[0]
    heads = up_ref.shape[1] // HD
    slot = 0
    for piece, parts in zip(pieces, blocks):
        at = 0
        for rows in parts:
            start = pl.multiple_of(offs_ref[slot], 16)
            qkv_ref[pl.ds(start, rows), :] = piece[at : at + rows, :]
            at += rows
            slot += 1
    scale = HD ** (-0.5)
    block = TILE
    k_at = heads * HD
    v_at = k_at + HD
    keys_t_ref[...] = qkv_ref[:, k_at:v_at].T
    dk_ref[...] = jnp.zeros_like(dk_ref)
    dv_ref[...] = jnp.zeros_like(dv_ref)
    across = (((1,), (1,)), ((), ()))

    def head(h, carry):
        cols = pl.ds(pl.multiple_of(h * HD, HD), HD)
        for r0 in range(0, seq, block):
            size = r0 + block
            keys = qkv_ref[:size, k_at:v_at]
            values = qkv_ref[:size, v_at : v_at + HD]
            row = lax.broadcasted_iota(jnp.int32, (block, size), 0) + r0
            col = lax.broadcasted_iota(jnp.int32, (block, size), 1)
            q = qkv_ref[r0:size, cols]
            up = up_ref[r0:size, cols]
            s = lax.dot_general(q, keys, across, preferred_element_type=F32)
            s = jnp.where(row >= col, s * scale, -1e30)
            p = jnp.exp(s - jnp.max(s, axis=1, keepdims=True))
            w = p * (1.0 / jnp.sum(p, axis=1, keepdims=True))
            dp = lax.dot_general(up, values, across, preferred_element_type=F32)
            delta = jnp.sum(w * dp, axis=1, keepdims=True)
            ds = (w * (dp - delta) * scale).astype(BF16)
            dq = lax.dot_general(keys_t_ref[:, :size], ds, across, preferred_element_type=F32)
            out_ref[cols, r0:size] = dq.astype(BF16)
            dk_ref[:, :size] += jnp.dot(q.T, ds, preferred_element_type=F32)
            dv_ref[:, :size] += jnp.dot(up.T, w.astype(BF16), preferred_element_type=F32)
        return carry

    lax.fori_loop(0, heads, head, 0)
    kv_ref[:HD, :] = dk_ref[...].astype(BF16)
    kv_ref[HD:, :] = dv_ref[...].astype(BF16)


def attention(pieces, blocks, offs, up):
    seq = up.shape[0]
    cols = pieces[0].shape[1]
    return pl.pallas_call(
        partial(attention_kernel, blocks),
        in_specs=[pl.BlockSpec(memory_space=pltpu.SMEM)] + [WHOLE] * (len(pieces) + 1),
        out_specs=[WHOLE] * 2,
        out_shape=[jax.ShapeDtypeStruct((n, seq), BF16) for n in (up.shape[1], cols - up.shape[1])],
        scratch_shapes=[
            pltpu.VMEM((seq, cols), BF16),
            pltpu.VMEM((HD, seq), BF16),
            pltpu.VMEM((HD, seq), F32),
            pltpu.VMEM((HD, seq), F32),
        ],
        compiler_params=PARAMS,
        cost_estimate=LIGHT,
        name="attention",
    )(offs, *pieces, up)


def grad_tile(offs_ref, pieces, depth, q_ref, kv_ref, rows_ref):
    for slot, piece in enumerate(pieces):
        start = pl.multiple_of(offs_ref[slot], 16)
        rows_ref[pl.ds(start, piece.shape[0]), :] = piece[:, depth]
    dqkv = jnp.concatenate([q_ref[...], kv_ref[...]], axis=0)
    turned = jnp.dot(dqkv, rows_ref[...], preferred_element_type=F32)
    return turned.astype(BF16).T.astype(F32)


def over_tiles(width, tile, one):
    def pair(j, carry):
        for k in range(2):
            one(pl.ds(pl.multiple_of((2 * j + k) * tile, tile), tile), k)
        return carry

    lax.fori_loop(0, width // (2 * tile), pair, 0)


def own_grad_kernel(count, waits, offs_ref, *refs):
    pieces = refs[:count]
    q_ref, kv_ref, wq_ref, wk_ref, wv_ref, gain_ref = refs[count : count + 6]
    gq_ref, gk_ref, gv_ref, part_ref, rows_ref = refs[count + 6 + waits :]
    q_cols = gq_ref.shape[1]
    v_at = q_cols + gk_ref.shape[1]

    def one(depth, slot):
        grad = grad_tile(offs_ref, pieces, depth, q_ref, kv_ref, rows_ref.at[slot])
        gq_ref[depth, :] = grad[:, :q_cols].astype(BF16)
        gk_ref[depth, :] = grad[:, q_cols:v_at].astype(BF16)
        gv_ref[depth, :] = grad[:, v_at:].astype(BF16)
        folded = grad[:, q_cols:v_at] * wk_ref[depth, :].astype(F32)
        folded = folded + grad[:, v_at:] * wv_ref[depth, :].astype(F32)
        for c in range(0, q_cols, HD):
            folded = folded + grad[:, c : c + HD] * wq_ref[depth, c : c + HD].astype(F32)
        total = jnp.sum(folded.T, axis=0, keepdims=True)
        part_ref[:, depth] = total / gain_ref[:, depth].astype(F32)

    over_tiles(gq_ref.shape[0], 2 * TILE, one)


def own_grad(pieces, offs, dqkv, wq, wk, wv, gain, earlier):
    seq = dqkv[0].shape[1]
    weights = (wq, wk, wv)
    outs = [jax.ShapeDtypeStruct(w.shape, BF16) for w in weights]
    return pl.pallas_call(
        partial(own_grad_kernel, len(pieces), len(earlier)),
        in_specs=[pl.BlockSpec(memory_space=pltpu.SMEM)]
        + [WHOLE] * (len(pieces) + 6 + len(earlier)),
        out_specs=[WHOLE] * 4,
        out_shape=outs + [jax.ShapeDtypeStruct((1, wq.shape[0]), F32)],
        scratch_shapes=[pltpu.VMEM((2, seq, 2 * TILE), BF16)],
        compiler_params=PARAMS,
        cost_estimate=LIGHT,
        name="own_grad",
    )(offs, *pieces, *dqkv, wq, wk, wv, gain, *earlier)


def peer_grad_kernel(count, offs_ref, *refs):
    pieces = refs[:count]
    q_ref, kv_ref, gq_ref, gk_ref, gv_ref, oq_ref, ok_ref, ov_ref, rows_ref = refs[count:]
    q_cols = gq_ref.shape[1]
    v_at = q_cols + gk_ref.shape[1]

    def one(depth, slot):
        grad = grad_tile(offs_ref, pieces, depth, q_ref, kv_ref, rows_ref.at[slot])
        oq_ref[depth, :] = (0.5 * (gq_ref[depth, :].astype(F32) + grad[:, :q_cols])).astype(BF16)
        ok_ref[depth, :] = (0.5 * (gk_ref[depth, :].astype(F32) + grad[:, q_cols:v_at])).astype(BF16)
        ov_ref[depth, :] = (0.5 * (gv_ref[depth, :].astype(F32) + grad[:, v_at:])).astype(BF16)

    over_tiles(gq_ref.shape[0], 2 * TILE, one)


def peer_grad(pieces, offs, dqkv, grads):
    seq = dqkv[0].shape[1]
    return pl.pallas_call(
        partial(peer_grad_kernel, len(pieces)),
        in_specs=[pl.BlockSpec(memory_space=pltpu.SMEM)]
        + [WHOLE] * (len(pieces) + len(dqkv) + 3),
        out_specs=[WHOLE] * 3,
        out_shape=[jax.ShapeDtypeStruct(g.shape, BF16) for g in grads],
        scratch_shapes=[pltpu.VMEM((2, seq, 2 * TILE), BF16)],
        compiler_params=PARAMS,
        cost_estimate=LIGHT,
        name="peer_grad",
    )(offs, *pieces, *dqkv, *grads)


def first_hop(own):
    return [from_tp(own, side) for side in ("left", "right", "pair")]


def second_hop(pair):
    return [from_tp(pair, "left"), from_tp(pair, "right")]


def third_hop(left, right_pair):
    return [from_tp(left, "left"), from_tp(right_pair, "right")]


def pair_sum(value):
    return value + from_tp(value, "pair")


def ring_sum(value):
    near, far, both = [
        lax.ppermute(value, "tp", [(i, i ^ (2 * apart)) for i in range(2 * X_RING)])
        for apart in (1, 2, 3)
    ]
    return (value + near) + (far + both)


def after(value, *earlier):
    return lax.optimization_barrier((value, *earlier))[0]


def exchange(peer_bit, *blocks):

    def branch(bit, operands):
        return [from_peer(block, bit) for block in operands]

    return lax.switch(peer_bit, [partial(branch, bit) for bit in range(4)], blocks)


def body(tokens, norm_gain, query_weight, key_weight, value_weight, grad_out, step_index):
    wq, wk, wv, up = query_weight[0], key_weight[0], value_weight[0], grad_out[0]
    peer_bit = jnp.mod(step_index, 4)
    normed, top, bottom = normalize(tokens[0], norm_gain)
    rows = normed.shape[0]
    places = [(0, 0), (-1, 0), (1, 0), (0, 1), (-1, 1), (1, 1), (2, 0), (2, 1)]
    offs = jnp.stack([offset_of(x, z, rows) for x, z in places]).astype(jnp.int32)

    first = first_hop(normed)
    second = second_hop(first[2])
    (peer_top,) = exchange(peer_bit, after(top, *first))
    left, right_pair = after((first[0], second[1]), peer_top)
    third = third_hop(left, right_pair)
    (peer_bottom,) = exchange(peer_bit, after(bottom, *second, peer_top))
    peer_own = join(peer_top, peer_bottom)
    peer_first = first_hop(after(peer_own, *third))
    rows_a = project(after([normed] + first, *third, peer_bottom), wq, wk, wv)
    rows_b = project(second + third, wq, wk, wv)
    blocks = [[rows] * 4] * 2
    dqkv = attention([rows_a, rows_b], blocks, offs, up)
    pieces = [normed] + first + second + third
    *grads, part = own_grad(pieces, offs, dqkv, wq, wk, wv, norm_gain, [])
    peer_second = second_hop(peer_first[2])
    paired = pair_sum(part)
    (peer_kv,) = exchange(peer_bit, after(dqkv[1], paired, *peer_first))
    grad_gain = ring_sum(after(paired, peer_kv, *peer_second)).astype(BF16)
    left, right_pair = after((peer_first[0], peer_second[1]), peer_kv)
    peer_third = third_hop(left, right_pair)
    peer_q, peer_gain = exchange(peer_bit, *after((dqkv[0], grad_gain), *peer_second))
    peer_pieces = [peer_own] + peer_first + peer_second + peer_third
    outs = peer_grad(peer_pieces, offs, [peer_q, peer_kv], grads)
    gain_update = (0.5 * (grad_gain.astype(F32) + peer_gain.astype(F32))).astype(BF16)
    return outs[0][None], outs[1][None], outs[2][None], gain_update


def solution(mesh):
    in_specs = (
        P("rep", "tp", None),
        P("rep", None),
        P("rep", None, "tp"),
        P("rep", None, "tp"),
        P("rep", None, "tp"),
        P("rep", None, "tp"),
        P(),
    )
    out_specs = (P("rep", None, "tp"), P("rep", None, "tp"), P("rep", None, "tp"), P("rep", None))
    return jax.shard_map(body, mesh=mesh, in_specs=in_specs, out_specs=out_specs, check_vma=False)
```

```python
from functools import partial

import jax
import jax.numpy as jnp
from jax import lax
from jax.experimental import pallas as pl
from jax.experimental.pallas import tpu as pltpu
from jax.sharding import PartitionSpec as P

HD = 128
EPS = 1e-05
X_RING = 4
F32 = jnp.float32
BF16 = jnp.bfloat16
VMEM_LIMIT = 16 * 1024 * 1024
TILE = 256
WHOLE = pl.BlockSpec(memory_space=pltpu.VMEM)
LIGHT = pl.CostEstimate(flops=1, bytes_accessed=1, transcendentals=0)
PARAMS = pltpu.CompilerParams(vmem_limit_bytes=VMEM_LIMIT)


def tp_of(x, z):
    return (x % X_RING) * 2 + z


ROUTES = {
    "left": [(tp_of(x, z), tp_of(x + 1, z)) for x in range(X_RING) for z in range(2)],
    "right": [(tp_of(x, z), tp_of(x - 1, z)) for x in range(X_RING) for z in range(2)],
    "pair": [(tp_of(x, z), tp_of(x, 1 - z)) for x in range(X_RING) for z in range(2)],
}


def from_tp(block, side):
    return lax.ppermute(block, "tp", ROUTES[side])


def from_peer(block, bit):
    count = lax.axis_size("rep")
    return lax.ppermute(block, "rep", [(r, r ^ (1 << bit)) for r in range(count)])


def offset_of(dx, dz, rows):
    index = lax.axis_index("tp")
    x, z = index // 2, index % 2
    return (((x + dx) % X_RING) * 2 + (z + dz) % 2) * rows


def norm_kernel(tokens_ref, gain_ref, out_ref, top_ref, bottom_ref):
    values = tokens_ref[...].astype(F32)
    mean_square = jnp.mean(values * values, axis=1, keepdims=True)
    unit = values * lax.rsqrt(mean_square + EPS)
    normed = (unit * gain_ref[...].astype(F32)).astype(BF16)
    half = top_ref.shape[0]
    out_ref[...] = normed
    top_ref[...] = normed[:half]
    bottom_ref[...] = normed[half:]


def normalize(tokens, gain):
    rows, width = tokens.shape
    shapes = [(rows, width), (rows // 2, width), (rows // 2, width)]
    return pl.pallas_call(
        norm_kernel,
        out_shape=[jax.ShapeDtypeStruct(shape, BF16) for shape in shapes],
        compiler_params=pltpu.CompilerParams(vmem_limit_bytes=VMEM_LIMIT),
        name="normalize",
    )(tokens, gain)


def join_kernel(top_ref, bottom_ref, out_ref):
    half = top_ref.shape[0]
    out_ref[:half, :] = top_ref[...]
    out_ref[half:, :] = bottom_ref[...]


def join(top, bottom):
    return pl.pallas_call(
        join_kernel,
        in_specs=[WHOLE] * 2,
        out_specs=WHOLE,
        out_shape=jax.ShapeDtypeStruct((2 * top.shape[0], top.shape[1]), BF16),
        compiler_params=PARAMS,
        cost_estimate=LIGHT,
        name="join",
    )(top, bottom)


def project_kernel(count, *refs):
    pieces = refs[:count]
    wq_ref, wk_ref, wv_ref, out_ref = refs[count:]
    q_cols = wq_ref.shape[1]
    tile = 1024
    q_sum = None
    kv_sum = None
    for at in range(0, wq_ref.shape[0], tile):
        depth = slice(at, at + tile)
        rows = [p[:, depth] for p in pieces]
        rows = jnp.concatenate(rows, axis=0) if count > 1 else rows[0]
        weight_kv = jnp.concatenate([wk_ref[depth, :], wv_ref[depth, :]], axis=1)
        q_part = jnp.dot(rows, wq_ref[depth, :], preferred_element_type=F32)
        kv_part = jnp.dot(rows, weight_kv, preferred_element_type=F32)
        q_sum = q_part if q_sum is None else q_sum + q_part
        kv_sum = kv_part if kv_sum is None else kv_sum + kv_part
    out_ref[:, :q_cols] = q_sum.astype(BF16)
    out_ref[:, q_cols:] = kv_sum.astype(BF16)


def project(pieces, wq, wk, wv):
    rows = sum(p.shape[0] for p in pieces)
    cols = wq.shape[1] + wk.shape[1] + wv.shape[1]
    return pl.pallas_call(
        partial(project_kernel, len(pieces)),
        in_specs=[WHOLE] * (len(pieces) + 3),
        out_specs=WHOLE,
        out_shape=jax.ShapeDtypeStruct((rows, cols), BF16),
        compiler_params=PARAMS,
        cost_estimate=LIGHT,
        name="project",
    )(*pieces, wq, wk, wv)


def attention_kernel(blocks, offs_ref, *refs):
    count = len(blocks)
    pieces = refs[:count]
    up_ref, out_ref, kv_ref, qkv_ref, keys_t_ref, dk_ref, dv_ref = refs[count:]
    seq = up_ref.shape[0]
    heads = up_ref.shape[1] // HD
    slot = 0
    for piece, parts in zip(pieces, blocks):
        at = 0
        for rows in parts:
            start = pl.multiple_of(offs_ref[slot], 16)
            qkv_ref[pl.ds(start, rows), :] = piece[at : at + rows, :]
            at += rows
            slot += 1
    scale = HD ** (-0.5)
    block = TILE
    k_at = heads * HD
    v_at = k_at + HD
    keys_t_ref[...] = qkv_ref[:, k_at:v_at].T
    dk_ref[...] = jnp.zeros_like(dk_ref)
    dv_ref[...] = jnp.zeros_like(dv_ref)
    across = (((1,), (1,)), ((), ()))

    def head(h, carry):
        cols = pl.ds(pl.multiple_of(h * HD, HD), HD)
        for r0 in range(0, seq, block):
            size = r0 + block
            keys = qkv_ref[:size, k_at:v_at]
            values = qkv_ref[:size, v_at : v_at + HD]
            row = lax.broadcasted_iota(jnp.int32, (block, size), 0) + r0
            col = lax.broadcasted_iota(jnp.int32, (block, size), 1)
            q = qkv_ref[r0:size, cols]
            up = up_ref[r0:size, cols]
            s = lax.dot_general(q, keys, across, preferred_element_type=F32)
            s = jnp.where(row >= col, s * scale, -1e30)
            p = jnp.exp(s - jnp.max(s, axis=1, keepdims=True))
            w = p * (1.0 / jnp.sum(p, axis=1, keepdims=True))
            dp = lax.dot_general(up, values, across, preferred_element_type=F32)
            delta = jnp.sum(w * dp, axis=1, keepdims=True)
            ds = (w * (dp - delta) * scale).astype(BF16)
            dq = lax.dot_general(keys_t_ref[:, :size], ds, across, preferred_element_type=F32)
            out_ref[cols, r0:size] = dq.astype(BF16)
            dk_ref[:, :size] += jnp.dot(q.T, ds, preferred_element_type=F32)
            dv_ref[:, :size] += jnp.dot(up.T, w.astype(BF16), preferred_element_type=F32)
        return carry

    lax.fori_loop(0, heads, head, 0)
    kv_ref[:HD, :] = dk_ref[...].astype(BF16)
    kv_ref[HD:, :] = dv_ref[...].astype(BF16)


def attention(pieces, blocks, offs, up):
    seq = up.shape[0]
    cols = pieces[0].shape[1]
    return pl.pallas_call(
        partial(attention_kernel, blocks),
        in_specs=[pl.BlockSpec(memory_space=pltpu.SMEM)] + [WHOLE] * (len(pieces) + 1),
        out_specs=[WHOLE] * 2,
        out_shape=[jax.ShapeDtypeStruct((n, seq), BF16) for n in (up.shape[1], cols - up.shape[1])],
        scratch_shapes=[
            pltpu.VMEM((seq, cols), BF16),
            pltpu.VMEM((HD, seq), BF16),
            pltpu.VMEM((HD, seq), F32),
            pltpu.VMEM((HD, seq), F32),
        ],
        compiler_params=PARAMS,
        cost_estimate=LIGHT,
        name="attention",
    )(offs, *pieces, up)


def grad_tile(offs_ref, pieces, depth, q_ref, kv_ref, rows_ref):
    for slot, piece in enumerate(pieces):
        start = pl.multiple_of(offs_ref[slot], 16)
        rows_ref[pl.ds(start, piece.shape[0]), :] = piece[:, depth]
    dqkv = jnp.concatenate([q_ref[...], kv_ref[...]], axis=0)
    turned = jnp.dot(dqkv, rows_ref[...], preferred_element_type=F32)
    return turned.astype(BF16).T.astype(F32)


def over_tiles(width, tile, one):
    def pair(j, carry):
        for k in range(2):
            index = 2 * j + k
            one(pl.ds(pl.multiple_of(index * tile, tile), tile), index, k)
        return carry

    lax.fori_loop(0, width // (2 * tile), pair, 0)


def own_grad_kernel(count, waits, offs_ref, *refs):
    pieces = refs[:count]
    q_ref, kv_ref, wq_ref, wk_ref, wv_ref, gain_ref = refs[count : count + 6]
    gq_ref, gk_ref, gv_ref, part_ref, rows_ref = refs[count + 6 + waits :]
    q_cols = gq_ref.shape[1]
    v_at = q_cols + gk_ref.shape[1]

    def one(depth, index, slot):
        grad = grad_tile(offs_ref, pieces, depth, q_ref, kv_ref, rows_ref.at[slot])
        gq_ref[depth, :] = grad[:, :q_cols].astype(BF16)
        gk_ref[depth, :] = grad[:, q_cols:v_at].astype(BF16)
        gv_ref[depth, :] = grad[:, v_at:].astype(BF16)
        folded = grad[:, q_cols:v_at] * wk_ref[depth, :].astype(F32)
        folded = folded + grad[:, v_at:] * wv_ref[depth, :].astype(F32)
        for c in range(0, q_cols, HD):
            folded = folded + grad[:, c : c + HD] * wq_ref[depth, c : c + HD].astype(F32)
        total = jnp.sum(folded.T, axis=0, keepdims=True)
        part_ref[:, depth] = total / gain_ref[:, depth].astype(F32)

    over_tiles(gq_ref.shape[0], 2 * TILE, one)


def own_grad(pieces, offs, dqkv, wq, wk, wv, gain, earlier):
    seq = dqkv[0].shape[1]
    weights = (wq, wk, wv)
    outs = [jax.ShapeDtypeStruct(w.shape, BF16) for w in weights]
    return pl.pallas_call(
        partial(own_grad_kernel, len(pieces), len(earlier)),
        in_specs=[pl.BlockSpec(memory_space=pltpu.SMEM)]
        + [WHOLE] * (len(pieces) + 6 + len(earlier)),
        out_specs=[WHOLE] * 4,
        out_shape=outs + [jax.ShapeDtypeStruct((1, wq.shape[0]), F32)],
        scratch_shapes=[pltpu.VMEM((2, seq, 2 * TILE), BF16)],
        compiler_params=PARAMS,
        cost_estimate=LIGHT,
        name="own_grad",
    )(offs, *pieces, *dqkv, wq, wk, wv, gain, *earlier)


def peer_grad_kernel(count, offs_ref, *refs):
    pieces = refs[:count]
    q_ref, kv_ref = refs[count : count + 2]
    own, outs, own_bufs, out_bufs = [refs[count + at : count + at + 3] for at in (2, 5, 8, 11)]
    rows_ref, in_sems, out_sems = refs[count + 14 :]
    tile = 2 * TILE
    width = own[0].shape[0]

    def fetch(n):
        return pltpu.make_async_copy(own[n], own_bufs[n], in_sems.at[n])

    def flush(n, depth, index):
        return pltpu.make_async_copy(
            out_bufs[n].at[depth, :], outs[n].at[depth, :], out_sems.at[index, n]
        )

    for n in range(3):
        fetch(n).start()

    def one(depth, index, slot):
        grad = grad_tile(offs_ref, pieces, depth, q_ref, kv_ref, rows_ref.at[slot])

        @pl.when(index == 0)
        def _():
            for n in range(3):
                fetch(n).wait()

        at = 0
        for n in range(3):
            cols = own_bufs[n].shape[1]
            mean = 0.5 * (own_bufs[n][depth, :].astype(F32) + grad[:, at : at + cols])
            out_bufs[n][depth, :] = mean.astype(BF16)
            flush(n, depth, index).start()
            at += cols

    over_tiles(width, tile, one)
    for index in range(width // tile):
        for n in range(3):
            flush(n, pl.ds(index * tile, tile), index).wait()


def peer_grad(pieces, offs, dqkv, grads):
    seq = dqkv[0].shape[1]
    width = grads[0].shape[0]
    anywhere = pl.BlockSpec(memory_space=pl.ANY)
    buffers = [pltpu.VMEM(g.shape, BF16) for g in grads]
    return pl.pallas_call(
        partial(peer_grad_kernel, len(pieces)),
        in_specs=[pl.BlockSpec(memory_space=pltpu.SMEM)]
        + [WHOLE] * (len(pieces) + 2)
        + [anywhere] * 3,
        out_specs=[anywhere] * 3,
        out_shape=[jax.ShapeDtypeStruct(g.shape, BF16) for g in grads],
        scratch_shapes=buffers
        + buffers
        + [
            pltpu.VMEM((2, seq, 2 * TILE), BF16),
            pltpu.SemaphoreType.DMA((3,)),
            pltpu.SemaphoreType.DMA((width // (2 * TILE), 3)),
        ],
        compiler_params=PARAMS,
        cost_estimate=LIGHT,
        name="peer_grad",
    )(offs, *pieces, *dqkv, *grads)


def first_hop(own):
    return [from_tp(own, side) for side in ("left", "right", "pair")]


def second_hop(pair):
    return [from_tp(pair, "left"), from_tp(pair, "right")]


def third_hop(left, right_pair):
    return [from_tp(left, "left"), from_tp(right_pair, "right")]


def pair_sum(value):
    return value + from_tp(value, "pair")


def ring_sum(value):
    near, far, both = [
        lax.ppermute(value, "tp", [(i, i ^ (2 * apart)) for i in range(2 * X_RING)])
        for apart in (1, 2, 3)
    ]
    return (value + near) + (far + both)


def after(value, *earlier):
    return lax.optimization_barrier((value, *earlier))[0]


def exchange(peer_bit, *blocks):

    def branch(bit, operands):
        return [from_peer(block, bit) for block in operands]

    return lax.switch(peer_bit, [partial(branch, bit) for bit in range(4)], blocks)


def body(tokens, norm_gain, query_weight, key_weight, value_weight, grad_out, step_index):
    wq, wk, wv, up = query_weight[0], key_weight[0], value_weight[0], grad_out[0]
    peer_bit = jnp.mod(step_index, 4)
    normed, top, bottom = normalize(tokens[0], norm_gain)
    rows = normed.shape[0]
    places = [(0, 0), (-1, 0), (1, 0), (0, 1), (-1, 1), (1, 1), (2, 0), (2, 1)]
    offs = jnp.stack([offset_of(x, z, rows) for x, z in places]).astype(jnp.int32)

    first = first_hop(normed)
    second = second_hop(first[2])
    (peer_top,) = exchange(peer_bit, after(top, *first))
    left, right_pair = after((first[0], second[1]), peer_top)
    third = third_hop(left, right_pair)
    rows_a = project([normed] + first, wq, wk, wv)
    (peer_bottom,) = exchange(peer_bit, after(bottom, *second, peer_top, rows_a))
    peer_own = join(peer_top, peer_bottom)
    peer_first = first_hop(after(peer_own, *third))
    rows_b = project(second + third, wq, wk, wv)
    blocks = [[rows] * 4] * 2
    dqkv = attention([rows_a, rows_b], blocks, offs, up)
    pieces = [normed] + first + second + third
    *grads, part = own_grad(pieces, offs, dqkv, wq, wk, wv, norm_gain, [])
    peer_second = second_hop(after(peer_first[2], part))
    paired = pair_sum(part)
    (peer_kv,) = exchange(peer_bit, after(dqkv[1], paired, *peer_first))
    grad_gain = ring_sum(after(paired, peer_kv, *peer_second)).astype(BF16)
    left, right_pair = after((peer_first[0], peer_second[1]), peer_kv)
    peer_third = third_hop(left, right_pair)
    peer_q, peer_gain = exchange(peer_bit, *after((dqkv[0], grad_gain), *peer_second))
    peer_pieces = [peer_own] + peer_first + peer_second + peer_third
    outs = peer_grad(peer_pieces, offs, [peer_q, peer_kv], grads)
    gain_update = (0.5 * (grad_gain.astype(F32) + peer_gain.astype(F32))).astype(BF16)
    return outs[0][None], outs[1][None], outs[2][None], gain_update


def solution(mesh):
    in_specs = (
        P("rep", "tp", None),
        P("rep", None),
        P("rep", None, "tp"),
        P("rep", None, "tp"),
        P("rep", None, "tp"),
        P("rep", None, "tp"),
        P(),
    )
    out_specs = (P("rep", None, "tp"), P("rep", None, "tp"), P("rep", None, "tp"), P("rep", None))
    return jax.shard_map(body, mesh=mesh, in_specs=in_specs, out_specs=out_specs, check_vma=False)
```

```python
from functools import partial

import jax
import jax.numpy as jnp
from jax import lax
from jax.experimental import pallas as pl
from jax.experimental.pallas import tpu as pltpu
from jax.sharding import PartitionSpec as P

HD = 128
EPS = 1e-05
X_RING = 4
F32 = jnp.float32
BF16 = jnp.bfloat16
VMEM_LIMIT = 16 * 1024 * 1024
TILE = 256
WHOLE = pl.BlockSpec(memory_space=pltpu.VMEM)
IN_HBM = pl.BlockSpec(memory_space=pltpu.HBM)
LIGHT = pl.CostEstimate(flops=1, bytes_accessed=1, transcendentals=0)
PARAMS = pltpu.CompilerParams(vmem_limit_bytes=VMEM_LIMIT)


def tp_of(x, z):
    return (x % X_RING) * 2 + z


ROUTES = {
    "left": [(tp_of(x, z), tp_of(x + 1, z)) for x in range(X_RING) for z in range(2)],
    "right": [(tp_of(x, z), tp_of(x - 1, z)) for x in range(X_RING) for z in range(2)],
    "pair": [(tp_of(x, z), tp_of(x, 1 - z)) for x in range(X_RING) for z in range(2)],
}


def from_tp(block, side):
    return lax.ppermute(block, "tp", ROUTES[side])


def from_peer(block, bit):
    count = lax.axis_size("rep")
    return lax.ppermute(block, "rep", [(r, r ^ (1 << bit)) for r in range(count)])


def offset_of(dx, dz, rows):
    index = lax.axis_index("tp")
    x, z = index // 2, index % 2
    return (((x + dx) % X_RING) * 2 + (z + dz) % 2) * rows


def norm_kernel(tokens_ref, gain_ref, out_ref, top_ref, bottom_ref):
    values = tokens_ref[...].astype(F32)
    mean_square = jnp.mean(values * values, axis=1, keepdims=True)
    unit = values * lax.rsqrt(mean_square + EPS)
    normed = (unit * gain_ref[...].astype(F32)).astype(BF16)
    half = top_ref.shape[0]
    out_ref[...] = normed
    top_ref[...] = normed[:half]
    bottom_ref[...] = normed[half:]


def normalize(tokens, gain):
    rows, width = tokens.shape
    shapes = [(rows, width), (rows // 2, width), (rows // 2, width)]
    return pl.pallas_call(
        norm_kernel,
        out_shape=[jax.ShapeDtypeStruct(shape, BF16) for shape in shapes],
        compiler_params=pltpu.CompilerParams(vmem_limit_bytes=VMEM_LIMIT),
        name="normalize",
    )(tokens, gain)


def join_kernel(top_ref, bottom_ref, out_ref):
    half = top_ref.shape[0]
    out_ref[:half, :] = top_ref[...]
    out_ref[half:, :] = bottom_ref[...]


def join(top, bottom):
    return pl.pallas_call(
        join_kernel,
        in_specs=[WHOLE] * 2,
        out_specs=WHOLE,
        out_shape=jax.ShapeDtypeStruct((2 * top.shape[0], top.shape[1]), BF16),
        compiler_params=PARAMS,
        cost_estimate=LIGHT,
        name="join",
    )(top, bottom)


def project_kernel(count, *refs):
    pieces = refs[:count]
    wq_ref, wk_ref, wv_ref, out_ref = refs[count:]
    q_cols = wq_ref.shape[1]
    tile = 1024
    q_sum = None
    kv_sum = None
    for at in range(0, wq_ref.shape[0], tile):
        depth = slice(at, at + tile)
        rows = [p[:, depth] for p in pieces]
        rows = jnp.concatenate(rows, axis=0) if count > 1 else rows[0]
        weight_kv = jnp.concatenate([wk_ref[depth, :], wv_ref[depth, :]], axis=1)
        q_part = jnp.dot(rows, wq_ref[depth, :], preferred_element_type=F32)
        kv_part = jnp.dot(rows, weight_kv, preferred_element_type=F32)
        q_sum = q_part if q_sum is None else q_sum + q_part
        kv_sum = kv_part if kv_sum is None else kv_sum + kv_part
    out_ref[:, :q_cols] = q_sum.astype(BF16)
    out_ref[:, q_cols:] = kv_sum.astype(BF16)


def project(pieces, wq, wk, wv):
    rows = sum(p.shape[0] for p in pieces)
    cols = wq.shape[1] + wk.shape[1] + wv.shape[1]
    return pl.pallas_call(
        partial(project_kernel, len(pieces)),
        in_specs=[WHOLE] * (len(pieces) + 3),
        out_specs=WHOLE,
        out_shape=jax.ShapeDtypeStruct((rows, cols), BF16),
        compiler_params=PARAMS,
        cost_estimate=LIGHT,
        name="project",
    )(*pieces, wq, wk, wv)


def attention_kernel(blocks, offs_ref, *refs):
    count = len(blocks)
    pieces = refs[:count]
    up_ref, out_ref, kv_ref, qkv_ref, keys_t_ref, dk_ref, dv_ref = refs[count:]
    seq = up_ref.shape[0]
    heads = up_ref.shape[1] // HD
    slot = 0
    for piece, parts in zip(pieces, blocks):
        at = 0
        for rows in parts:
            start = pl.multiple_of(offs_ref[slot], 16)
            qkv_ref[pl.ds(start, rows), :] = piece[at : at + rows, :]
            at += rows
            slot += 1
    scale = HD ** (-0.5)
    block = TILE
    k_at = heads * HD
    v_at = k_at + HD
    keys_t_ref[...] = qkv_ref[:, k_at:v_at].T
    dk_ref[...] = jnp.zeros_like(dk_ref)
    dv_ref[...] = jnp.zeros_like(dv_ref)
    across = (((1,), (1,)), ((), ()))

    def head(h, carry):
        cols = pl.ds(pl.multiple_of(h * HD, HD), HD)
        for r0 in range(0, seq, block):
            size = r0 + block
            keys = qkv_ref[:size, k_at:v_at]
            values = qkv_ref[:size, v_at : v_at + HD]
            row = lax.broadcasted_iota(jnp.int32, (block, size), 0) + r0
            col = lax.broadcasted_iota(jnp.int32, (block, size), 1)
            q = qkv_ref[r0:size, cols]
            up = up_ref[r0:size, cols]
            s = lax.dot_general(q, keys, across, preferred_element_type=F32)
            s = jnp.where(row >= col, s * scale, -1e30)
            p = jnp.exp(s - jnp.max(s, axis=1, keepdims=True))
            w = p * (1.0 / jnp.sum(p, axis=1, keepdims=True))
            dp = lax.dot_general(up, values, across, preferred_element_type=F32)
            delta = jnp.sum(w * dp, axis=1, keepdims=True)
            ds = (w * (dp - delta) * scale).astype(BF16)
            dq = lax.dot_general(keys_t_ref[:, :size], ds, across, preferred_element_type=F32)
            out_ref[cols, r0:size] = dq.astype(BF16)
            dk_ref[:, :size] += jnp.dot(q.T, ds, preferred_element_type=F32)
            dv_ref[:, :size] += jnp.dot(up.T, w.astype(BF16), preferred_element_type=F32)
        return carry

    lax.fori_loop(0, heads, head, 0)
    kv_ref[:HD, :] = dk_ref[...].astype(BF16)
    kv_ref[HD:, :] = dv_ref[...].astype(BF16)


def attention(pieces, blocks, offs, up):
    seq = up.shape[0]
    cols = pieces[0].shape[1]
    return pl.pallas_call(
        partial(attention_kernel, blocks),
        in_specs=[pl.BlockSpec(memory_space=pltpu.SMEM)] + [WHOLE] * (len(pieces) + 1),
        out_specs=[WHOLE] * 2,
        out_shape=[jax.ShapeDtypeStruct((n, seq), BF16) for n in (up.shape[1], cols - up.shape[1])],
        scratch_shapes=[
            pltpu.VMEM((seq, cols), BF16),
            pltpu.VMEM((HD, seq), BF16),
            pltpu.VMEM((HD, seq), F32),
            pltpu.VMEM((HD, seq), F32),
        ],
        compiler_params=PARAMS,
        cost_estimate=LIGHT,
        name="attention",
    )(offs, *pieces, up)


def grad_tile(offs_ref, pieces, depth, q_ref, kv_ref, rows_ref):
    for slot, piece in enumerate(pieces):
        start = pl.multiple_of(offs_ref[slot], 16)
        rows_ref[pl.ds(start, piece.shape[0]), :] = piece[:, depth]
    dqkv = jnp.concatenate([q_ref[...], kv_ref[...]], axis=0)
    turned = jnp.dot(dqkv, rows_ref[...], preferred_element_type=F32)
    return turned.astype(BF16).T.astype(F32)


def flush(buffers, outs, sems, tile, index):
    depth = pl.ds(index * tile, tile)
    return [
        pltpu.make_async_copy(buf.at[depth, :], out.at[depth, :], sems.at[index, n])
        for n, (buf, out) in enumerate(zip(buffers, outs))
    ]


def own_grad_kernel(count, offs_ref, *refs):
    pieces = refs[:count]
    q_ref, kv_ref, wq_ref, wk_ref, wv_ref, gain_ref = refs[count : count + 6]
    outs = refs[count + 6 : count + 9]
    part_ref = refs[count + 9]
    buffers = refs[count + 10 : count + 13]
    rows_ref, sems = refs[count + 13 :]
    tile = 2 * TILE
    tiles = wq_ref.shape[0] // tile
    for index in range(tiles):
        depth = slice(index * tile, (index + 1) * tile)
        grad = grad_tile(offs_ref, pieces, depth, q_ref, kv_ref, rows_ref.at[index % 2])
        folded = None
        at = 0
        for buf, weight in zip(buffers, (wq_ref, wk_ref, wv_ref)):
            cols = buf.shape[1]
            buf[depth, :] = grad[:, at : at + cols].astype(BF16)
            for c in range(0, cols, HD):
                term = grad[:, at + c : at + c + HD] * weight[depth, c : c + HD].astype(F32)
                folded = term if folded is None else folded + term
            at += cols
        for copy in flush(buffers, outs, sems, tile, index):
            copy.start()
        total = jnp.sum(folded.T, axis=0, keepdims=True)
        part_ref[:, depth] = total / gain_ref[:, depth].astype(F32)
    for index in range(tiles):
        for copy in flush(buffers, outs, sems, tile, index):
            copy.wait()


def own_grad(pieces, offs, dqkv, wq, wk, wv, gain):
    seq = dqkv[0].shape[1]
    weights = (wq, wk, wv)
    width = wq.shape[0]
    return pl.pallas_call(
        partial(own_grad_kernel, len(pieces)),
        in_specs=[pl.BlockSpec(memory_space=pltpu.SMEM)] + [WHOLE] * (len(pieces) + 6),
        out_specs=[IN_HBM] * 3 + [WHOLE],
        out_shape=[jax.ShapeDtypeStruct(w.shape, BF16) for w in weights]
        + [jax.ShapeDtypeStruct((1, width), F32)],
        scratch_shapes=[pltpu.VMEM(w.shape, BF16) for w in weights]
        + [
            pltpu.VMEM((2, seq, 2 * TILE), BF16),
            pltpu.SemaphoreType.DMA((width // (2 * TILE), 3)),
        ],
        compiler_params=PARAMS,
        cost_estimate=LIGHT,
        name="own_grad",
    )(offs, *pieces, *dqkv, wq, wk, wv, gain)


def peer_grad_kernel(count, offs_ref, *refs):
    pieces = refs[:count]
    q_ref, kv_ref = refs[count : count + 2]
    own, outs, own_bufs, out_bufs = [refs[count + at : count + at + 3] for at in (2, 5, 8, 11)]
    rows_ref, in_sems, out_sems = refs[count + 14 :]
    tile = 2 * TILE
    tiles = own[0].shape[0] // tile
    fetches = [pltpu.make_async_copy(own[n], own_bufs[n], in_sems.at[n]) for n in range(3)]
    for fetch in fetches:
        fetch.start()
    for index in range(tiles):
        depth = slice(index * tile, (index + 1) * tile)
        grad = grad_tile(offs_ref, pieces, depth, q_ref, kv_ref, rows_ref.at[index % 2])
        if index == 0:
            for fetch in fetches:
                fetch.wait()
        at = 0
        for mine, out in zip(own_bufs, out_bufs):
            cols = mine.shape[1]
            mean = 0.5 * (mine[depth, :].astype(F32) + grad[:, at : at + cols])
            out[depth, :] = mean.astype(BF16)
            at += cols
        for copy in flush(out_bufs, outs, out_sems, tile, index):
            copy.start()
    for index in range(tiles):
        for copy in flush(out_bufs, outs, out_sems, tile, index):
            copy.wait()


def peer_grad(pieces, offs, dqkv, grads):
    seq = dqkv[0].shape[1]
    width = grads[0].shape[0]
    buffers = [pltpu.VMEM(g.shape, BF16) for g in grads]
    return pl.pallas_call(
        partial(peer_grad_kernel, len(pieces)),
        in_specs=[pl.BlockSpec(memory_space=pltpu.SMEM)]
        + [WHOLE] * (len(pieces) + 2)
        + [IN_HBM] * 3,
        out_specs=[IN_HBM] * 3,
        out_shape=[jax.ShapeDtypeStruct(g.shape, BF16) for g in grads],
        scratch_shapes=buffers
        + buffers
        + [
            pltpu.VMEM((2, seq, 2 * TILE), BF16),
            pltpu.SemaphoreType.DMA((3,)),
            pltpu.SemaphoreType.DMA((width // (2 * TILE), 3)),
        ],
        compiler_params=PARAMS,
        cost_estimate=LIGHT,
        name="peer_grad",
    )(offs, *pieces, *dqkv, *grads)


def first_hop(own):
    return [from_tp(own, side) for side in ("left", "right", "pair")]


def second_hop(pair):
    return [from_tp(pair, "left"), from_tp(pair, "right")]


def third_hop(left, right_pair):
    return [from_tp(left, "left"), from_tp(right_pair, "right")]


def pair_sum(value):
    return value + from_tp(value, "pair")


def ring_sum(value):
    near, far, both = [
        lax.ppermute(value, "tp", [(i, i ^ (2 * apart)) for i in range(2 * X_RING)])
        for apart in (1, 2, 3)
    ]
    return (value + near) + (far + both)


def after(value, *earlier):
    return lax.optimization_barrier((value, *earlier))[0]


def exchange(peer_bit, *blocks):

    def branch(bit, operands):
        return [from_peer(block, bit) for block in operands]

    return lax.switch(peer_bit, [partial(branch, bit) for bit in range(4)], blocks)


def body(tokens, norm_gain, query_weight, key_weight, value_weight, grad_out, step_index):
    wq, wk, wv, up = query_weight[0], key_weight[0], value_weight[0], grad_out[0]
    peer_bit = jnp.mod(step_index, 4)
    normed, top, bottom = normalize(tokens[0], norm_gain)
    rows = normed.shape[0]
    places = [(0, 0), (-1, 0), (1, 0), (0, 1), (-1, 1), (1, 1), (2, 0), (2, 1)]
    offs = jnp.stack([offset_of(x, z, rows) for x, z in places]).astype(jnp.int32)

    first = first_hop(normed)
    second = second_hop(first[2])
    (peer_top,) = exchange(peer_bit, after(top, *first))
    left, right_pair = after((first[0], second[1]), peer_top)
    third = third_hop(left, right_pair)
    rows_a = project([normed] + first, wq, wk, wv)
    (peer_bottom,) = exchange(peer_bit, after(bottom, *second, peer_top, rows_a))
    peer_own = join(peer_top, peer_bottom)
    peer_first = first_hop(after(peer_own, *third))
    rows_b = project(second + third, wq, wk, wv)
    blocks = [[rows] * 4] * 2
    dqkv = attention([rows_a, rows_b], blocks, offs, up)
    pieces = [normed] + first + second + third
    *grads, part = own_grad(pieces, offs, dqkv, wq, wk, wv, norm_gain)
    peer_second = second_hop(after(peer_first[2], part))
    paired = pair_sum(part)
    (peer_kv,) = exchange(peer_bit, after(dqkv[1], paired, *peer_first))
    grad_gain = ring_sum(after(paired, peer_kv, *peer_second)).astype(BF16)
    left, right_pair = after((peer_first[0], peer_second[1]), peer_kv)
    peer_third = third_hop(left, right_pair)
    peer_q, peer_gain = exchange(peer_bit, *after((dqkv[0], grad_gain), *peer_second))
    peer_pieces = [peer_own] + peer_first + peer_second + peer_third
    outs = peer_grad(peer_pieces, offs, [peer_q, peer_kv], grads)
    gain_update = (0.5 * (grad_gain.astype(F32) + peer_gain.astype(F32))).astype(BF16)
    return outs[0][None], outs[1][None], outs[2][None], gain_update


def solution(mesh):
    in_specs = (
        P("rep", "tp", None),
        P("rep", None),
        P("rep", None, "tp"),
        P("rep", None, "tp"),
        P("rep", None, "tp"),
        P("rep", None, "tp"),
        P(),
    )
    out_specs = (P("rep", None, "tp"), P("rep", None, "tp"), P("rep", None, "tp"), P("rep", None))
    return jax.shard_map(body, mesh=mesh, in_specs=in_specs, out_specs=out_specs, check_vma=False)
```

```python
from functools import partial

import jax
import jax.numpy as jnp
from jax import lax
from jax.experimental import pallas as pl
from jax.experimental.pallas import tpu as pltpu
from jax.sharding import PartitionSpec as P

HD = 128
EPS = 1e-05
X_RING = 4
F32 = jnp.float32
BF16 = jnp.bfloat16
VMEM_LIMIT = 16 * 1024 * 1024
TILE = 256
WHOLE = pl.BlockSpec(memory_space=pltpu.VMEM)
IN_HBM = pl.BlockSpec(memory_space=pltpu.HBM)
LIGHT = pl.CostEstimate(flops=1, bytes_accessed=1, transcendentals=0)
PARAMS = pltpu.CompilerParams(vmem_limit_bytes=VMEM_LIMIT)
OWN_PARAMS = pltpu.CompilerParams(vmem_limit_bytes=50 * 1024 * 1024)
PEER_PARAMS = pltpu.CompilerParams(vmem_limit_bytes=53 * 1024 * 1024)


def tp_of(x, z):
    return (x % X_RING) * 2 + z


ROUTES = {
    "left": [(tp_of(x, z), tp_of(x + 1, z)) for x in range(X_RING) for z in range(2)],
    "right": [(tp_of(x, z), tp_of(x - 1, z)) for x in range(X_RING) for z in range(2)],
    "pair": [(tp_of(x, z), tp_of(x, 1 - z)) for x in range(X_RING) for z in range(2)],
}


def from_tp(block, side):
    return lax.ppermute(block, "tp", ROUTES[side])


def from_peer(block, bit):
    count = lax.axis_size("rep")
    return lax.ppermute(block, "rep", [(r, r ^ (1 << bit)) for r in range(count)])


def offset_of(dx, dz, rows):
    index = lax.axis_index("tp")
    x, z = index // 2, index % 2
    return (((x + dx) % X_RING) * 2 + (z + dz) % 2) * rows


def norm_kernel(tokens_ref, gain_ref, out_ref, top_ref, bottom_ref):
    values = tokens_ref[...].astype(F32)
    mean_square = jnp.mean(values * values, axis=1, keepdims=True)
    unit = values * lax.rsqrt(mean_square + EPS)
    normed = (unit * gain_ref[...].astype(F32)).astype(BF16)
    half = top_ref.shape[0]
    out_ref[...] = normed
    top_ref[...] = normed[:half]
    bottom_ref[...] = normed[half:]


def normalize(tokens, gain):
    rows, width = tokens.shape
    shapes = [(rows, width), (rows // 2, width), (rows // 2, width)]
    return pl.pallas_call(
        norm_kernel,
        out_shape=[jax.ShapeDtypeStruct(shape, BF16) for shape in shapes],
        compiler_params=pltpu.CompilerParams(vmem_limit_bytes=VMEM_LIMIT),
        name="normalize",
    )(tokens, gain)


def join_kernel(top_ref, bottom_ref, out_ref):
    half = top_ref.shape[0]
    out_ref[:half, :] = top_ref[...]
    out_ref[half:, :] = bottom_ref[...]


def join(top, bottom):
    return pl.pallas_call(
        join_kernel,
        in_specs=[WHOLE] * 2,
        out_specs=WHOLE,
        out_shape=jax.ShapeDtypeStruct((2 * top.shape[0], top.shape[1]), BF16),
        compiler_params=PARAMS,
        cost_estimate=LIGHT,
        name="join",
    )(top, bottom)


def project_kernel(count, *refs):
    pieces = refs[:count]
    wq_ref, wk_ref, wv_ref, out_ref = refs[count:]
    q_cols = wq_ref.shape[1]
    tile = 1024
    q_sum = None
    kv_sum = None
    for at in range(0, wq_ref.shape[0], tile):
        depth = slice(at, at + tile)
        rows = [p[:, depth] for p in pieces]
        rows = jnp.concatenate(rows, axis=0) if count > 1 else rows[0]
        weight_kv = jnp.concatenate([wk_ref[depth, :], wv_ref[depth, :]], axis=1)
        q_part = jnp.dot(rows, wq_ref[depth, :], preferred_element_type=F32)
        kv_part = jnp.dot(rows, weight_kv, preferred_element_type=F32)
        q_sum = q_part if q_sum is None else q_sum + q_part
        kv_sum = kv_part if kv_sum is None else kv_sum + kv_part
    out_ref[:, :q_cols] = q_sum.astype(BF16)
    out_ref[:, q_cols:] = kv_sum.astype(BF16)


def project(pieces, wq, wk, wv):
    rows = sum(p.shape[0] for p in pieces)
    cols = wq.shape[1] + wk.shape[1] + wv.shape[1]
    return pl.pallas_call(
        partial(project_kernel, len(pieces)),
        in_specs=[WHOLE] * (len(pieces) + 3),
        out_specs=WHOLE,
        out_shape=jax.ShapeDtypeStruct((rows, cols), BF16),
        compiler_params=PARAMS,
        cost_estimate=LIGHT,
        name="project",
    )(*pieces, wq, wk, wv)


def attention_kernel(blocks, offs_ref, *refs):
    count = len(blocks)
    pieces = refs[:count]
    up_ref, out_ref, kv_ref, qkv_ref, keys_t_ref, dk_ref, dv_ref = refs[count:]
    seq = up_ref.shape[0]
    heads = up_ref.shape[1] // HD
    slot = 0
    for piece, parts in zip(pieces, blocks):
        at = 0
        for rows in parts:
            start = pl.multiple_of(offs_ref[slot], 16)
            qkv_ref[pl.ds(start, rows), :] = piece[at : at + rows, :]
            at += rows
            slot += 1
    scale = HD ** (-0.5)
    block = TILE
    k_at = heads * HD
    v_at = k_at + HD
    keys_t_ref[...] = qkv_ref[:, k_at:v_at].T
    dk_ref[...] = jnp.zeros_like(dk_ref)
    dv_ref[...] = jnp.zeros_like(dv_ref)
    across = (((1,), (1,)), ((), ()))

    def head(h, carry):
        cols = pl.ds(pl.multiple_of(h * HD, HD), HD)
        for r0 in range(0, seq, block):
            size = r0 + block
            keys = qkv_ref[:size, k_at:v_at]
            values = qkv_ref[:size, v_at : v_at + HD]
            row = lax.broadcasted_iota(jnp.int32, (block, size), 0) + r0
            col = lax.broadcasted_iota(jnp.int32, (block, size), 1)
            q = qkv_ref[r0:size, cols]
            up = up_ref[r0:size, cols]
            s = lax.dot_general(q, keys, across, preferred_element_type=F32)
            s = jnp.where(row >= col, s * scale, -1e30)
            p = jnp.exp(s - jnp.max(s, axis=1, keepdims=True))
            w = p * (1.0 / jnp.sum(p, axis=1, keepdims=True))
            dp = lax.dot_general(up, values, across, preferred_element_type=F32)
            delta = jnp.sum(w * dp, axis=1, keepdims=True)
            ds = (w * (dp - delta) * scale).astype(BF16)
            dq = lax.dot_general(keys_t_ref[:, :size], ds, across, preferred_element_type=F32)
            out_ref[cols, r0:size] = dq.astype(BF16)
            dk_ref[:, :size] += jnp.dot(q.T, ds, preferred_element_type=F32)
            dv_ref[:, :size] += jnp.dot(up.T, w.astype(BF16), preferred_element_type=F32)
        return carry

    lax.fori_loop(0, heads, head, 0)
    kv_ref[:HD, :] = dk_ref[...].astype(BF16)
    kv_ref[HD:, :] = dv_ref[...].astype(BF16)


def attention(pieces, blocks, offs, up):
    seq = up.shape[0]
    cols = pieces[0].shape[1]
    return pl.pallas_call(
        partial(attention_kernel, blocks),
        in_specs=[pl.BlockSpec(memory_space=pltpu.SMEM)] + [WHOLE] * (len(pieces) + 1),
        out_specs=[WHOLE] * 2,
        out_shape=[jax.ShapeDtypeStruct((n, seq), BF16) for n in (up.shape[1], cols - up.shape[1])],
        scratch_shapes=[
            pltpu.VMEM((seq, cols), BF16),
            pltpu.VMEM((HD, seq), BF16),
            pltpu.VMEM((HD, seq), F32),
            pltpu.VMEM((HD, seq), F32),
        ],
        compiler_params=PARAMS,
        cost_estimate=LIGHT,
        name="attention",
    )(offs, *pieces, up)


def grad_tile(offs_ref, pieces, depth, q_ref, kv_ref, rows_ref):
    for slot, piece in enumerate(pieces):
        start = pl.multiple_of(offs_ref[slot], 16)
        rows_ref[pl.ds(start, piece.shape[0]), :] = piece[:, depth]
    dqkv = jnp.concatenate([q_ref[...], kv_ref[...]], axis=0)
    turned = jnp.dot(dqkv, rows_ref[...], preferred_element_type=F32)
    return turned.astype(BF16).T.astype(F32)


def flush(buffers, outs, sems, tile, index):
    depth = pl.ds(index * tile, tile)
    return [
        pltpu.make_async_copy(buf.at[depth, :], out.at[depth, :], sems.at[index, n])
        for n, (buf, out) in enumerate(zip(buffers, outs))
    ]


def own_grad_kernel(count, offs_ref, *refs):
    pieces = refs[:count]
    q_ref, kv_ref, wq_ref, wk_ref, wv_ref, gain_ref = refs[count : count + 6]
    outs = refs[count + 6 : count + 9]
    part_ref = refs[count + 9]
    buffers = refs[count + 10 : count + 13]
    rows_ref, sems = refs[count + 13 :]
    tile = 2 * TILE
    tiles = wq_ref.shape[0] // tile
    for index in range(tiles):
        depth = slice(index * tile, (index + 1) * tile)
        grad = grad_tile(offs_ref, pieces, depth, q_ref, kv_ref, rows_ref.at[index % 2])
        folded = None
        at = 0
        for buf, weight in zip(buffers, (wq_ref, wk_ref, wv_ref)):
            cols = buf.shape[1]
            buf[depth, :] = grad[:, at : at + cols].astype(BF16)
            for c in range(0, cols, HD):
                term = grad[:, at + c : at + c + HD] * weight[depth, c : c + HD].astype(F32)
                folded = term if folded is None else folded + term
            at += cols
        for copy in flush(buffers, outs, sems, tile, index):
            copy.start()
        total = jnp.sum(folded.T, axis=0, keepdims=True)
        part_ref[:, depth] = total / gain_ref[:, depth].astype(F32)
    for index in range(tiles):
        for copy in flush(buffers, outs, sems, tile, index):
            copy.wait()


def own_grad(pieces, offs, dqkv, wq, wk, wv, gain):
    seq = dqkv[0].shape[1]
    weights = (wq, wk, wv)
    width = wq.shape[0]
    return pl.pallas_call(
        partial(own_grad_kernel, len(pieces)),
        in_specs=[pl.BlockSpec(memory_space=pltpu.SMEM)] + [WHOLE] * (len(pieces) + 6),
        out_specs=[IN_HBM] * 3 + [WHOLE],
        out_shape=[jax.ShapeDtypeStruct(w.shape, BF16) for w in weights]
        + [jax.ShapeDtypeStruct((1, width), F32)],
        scratch_shapes=[pltpu.VMEM(w.shape, BF16) for w in weights]
        + [
            pltpu.VMEM((2, seq, 2 * TILE), BF16),
            pltpu.SemaphoreType.DMA((width // (2 * TILE), 3)),
        ],
        compiler_params=OWN_PARAMS,
        cost_estimate=LIGHT,
        name="own_grad",
    )(offs, *pieces, *dqkv, wq, wk, wv, gain)


def peer_grad_kernel(count, offs_ref, *refs):
    pieces = refs[:count]
    q_ref, kv_ref = refs[count : count + 2]
    own, outs, own_bufs, out_bufs = [refs[count + at : count + at + 3] for at in (2, 5, 8, 11)]
    rows_ref, in_sems, out_sems = refs[count + 14 :]
    tile = 2 * TILE
    tiles = own[0].shape[0] // tile
    fetches = [pltpu.make_async_copy(own[n], own_bufs[n], in_sems.at[n]) for n in range(3)]
    for fetch in fetches:
        fetch.start()
    for index in range(tiles):
        depth = slice(index * tile, (index + 1) * tile)
        grad = grad_tile(offs_ref, pieces, depth, q_ref, kv_ref, rows_ref.at[index % 2])
        if index == 0:
            for fetch in fetches:
                fetch.wait()
        at = 0
        for mine, out in zip(own_bufs, out_bufs):
            cols = mine.shape[1]
            mean = 0.5 * (mine[depth, :].astype(F32) + grad[:, at : at + cols])
            out[depth, :] = mean.astype(BF16)
            at += cols
        for copy in flush(out_bufs, outs, out_sems, tile, index):
            copy.start()
    for index in range(tiles):
        for copy in flush(out_bufs, outs, out_sems, tile, index):
            copy.wait()


def peer_grad(pieces, offs, dqkv, grads):
    seq = dqkv[0].shape[1]
    width = grads[0].shape[0]
    buffers = [pltpu.VMEM(g.shape, BF16) for g in grads]
    return pl.pallas_call(
        partial(peer_grad_kernel, len(pieces)),
        in_specs=[pl.BlockSpec(memory_space=pltpu.SMEM)]
        + [WHOLE] * (len(pieces) + 2)
        + [IN_HBM] * 3,
        out_specs=[IN_HBM] * 3,
        out_shape=[jax.ShapeDtypeStruct(g.shape, BF16) for g in grads],
        scratch_shapes=buffers
        + buffers
        + [
            pltpu.VMEM((2, seq, 2 * TILE), BF16),
            pltpu.SemaphoreType.DMA((3,)),
            pltpu.SemaphoreType.DMA((width // (2 * TILE), 3)),
        ],
        compiler_params=PEER_PARAMS,
        cost_estimate=LIGHT,
        name="peer_grad",
    )(offs, *pieces, *dqkv, *grads)


def first_hop(own):
    return [from_tp(own, side) for side in ("left", "right", "pair")]


def second_hop(pair):
    return [from_tp(pair, "left"), from_tp(pair, "right")]


def third_hop(left, right_pair):
    return [from_tp(left, "left"), from_tp(right_pair, "right")]


def pair_sum(value):
    return value + from_tp(value, "pair")


def ring_sum(value):
    near, far, both = [
        lax.ppermute(value, "tp", [(i, i ^ (2 * apart)) for i in range(2 * X_RING)])
        for apart in (1, 2, 3)
    ]
    return (value + near) + (far + both)


def after(value, *earlier):
    return lax.optimization_barrier((value, *earlier))[0]


def exchange(peer_bit, *blocks):

    def branch(bit, operands):
        return [from_peer(block, bit) for block in operands]

    return lax.switch(peer_bit, [partial(branch, bit) for bit in range(4)], blocks)


def body(tokens, norm_gain, query_weight, key_weight, value_weight, grad_out, step_index):
    wq, wk, wv, up = query_weight[0], key_weight[0], value_weight[0], grad_out[0]
    peer_bit = jnp.mod(step_index, 4)
    normed, top, bottom = normalize(tokens[0], norm_gain)
    rows = normed.shape[0]
    places = [(0, 0), (-1, 0), (1, 0), (0, 1), (-1, 1), (1, 1), (2, 0), (2, 1)]
    offs = jnp.stack([offset_of(x, z, rows) for x, z in places]).astype(jnp.int32)

    first = first_hop(normed)
    second = second_hop(first[2])
    (peer_top,) = exchange(peer_bit, after(top, *first))
    left, right_pair = after((first[0], second[1]), peer_top)
    third = third_hop(left, right_pair)
    rows_a = project([normed] + first, wq, wk, wv)
    (peer_bottom,) = exchange(peer_bit, after(bottom, *second, peer_top, rows_a))
    peer_own = join(peer_top, peer_bottom)
    peer_first = first_hop(after(peer_own, *third))
    rows_b = project(second + third, wq, wk, wv)
    blocks = [[rows] * 4] * 2
    dqkv = attention([rows_a, rows_b], blocks, offs, up)
    pieces = [normed] + first + second + third
    *grads, part = own_grad(pieces, offs, dqkv, wq, wk, wv, norm_gain)
    peer_second = second_hop(after(peer_first[2], part))
    paired = pair_sum(part)
    (peer_kv,) = exchange(peer_bit, after(dqkv[1], paired, *peer_first))
    grad_gain = ring_sum(after(paired, peer_kv, *peer_second)).astype(BF16)
    left, right_pair = after((peer_first[0], peer_second[1]), peer_kv)
    peer_third = third_hop(left, right_pair)
    peer_q, peer_gain = exchange(peer_bit, *after((dqkv[0], grad_gain), *peer_second))
    peer_pieces = [peer_own] + peer_first + peer_second + peer_third
    outs = peer_grad(peer_pieces, offs, [peer_q, peer_kv], grads)
    gain_update = (0.5 * (grad_gain.astype(F32) + peer_gain.astype(F32))).astype(BF16)
    return outs[0][None], outs[1][None], outs[2][None], gain_update


def solution(mesh):
    in_specs = (
        P("rep", "tp", None),
        P("rep", None),
        P("rep", None, "tp"),
        P("rep", None, "tp"),
        P("rep", None, "tp"),
        P("rep", None, "tp"),
        P(),
    )
    out_specs = (P("rep", None, "tp"), P("rep", None, "tp"), P("rep", None, "tp"), P("rep", None))
    return jax.shard_map(body, mesh=mesh, in_specs=in_specs, out_specs=out_specs, check_vma=False)
```
